256 devices in a mesh: row: 16 (over z, core), col: 4 (over y), depth: 4 (over x).
Axes of the slice: x: 4, y: 4, z: 8, core: 2. Of those that a mesh axis runs over, the one named last changes fastest.
Arguments:
- inputs: bfloat16 [8, 2048, 4096], P('depth', 'row', 'col'), may hold values from -12 to 12
- w_query: bfloat16 [4096, 2048], P('row', 'col'), may hold values from -0.109375 to 0.109375
- w_key: bfloat16 [4096, 512], P('row', 'col'), may hold values from -0.078125 to 0.078125
- w_value: bfloat16 [4096, 512], P('row', 'col'), may hold values from -0.09375 to 0.09375
- grad_out: bfloat16 [8, 2048, 2048], P('depth', 'row', 'col'), may hold values from -24 to 24
Outputs:
- grad_inputs: bfloat16 [8, 2048, 4096], P('depth', 'row', 'col')
- grad_query: float32 [4096, 2048], P(('row', 'depth'), 'col')
- grad_key: float32 [4096, 512], P(('row', 'depth'), 'col')
- grad_value: float32 [4096, 512], P(('row', 'depth'), 'col')
The draws below stay inside these ranges and needn't reach their ends.
All inputs are finite; a program needn't handle non-finite values.
Results may differ from the reference program's by a relative error of at most 0.028.
Values may be sent and summed in bfloat16 or wider, within the bound.
A program may use at most 128 MiB of HBM per device.

```python
import math
import jax
import jax.numpy as jnp
from jax import lax

D = 4096
HEADS = 16
KV_HEADS = 4
HEAD_DIM = 128
LEN = 2048
SEQS = 8


def key_base(key):
    return jax.random.truncated_normal(jax.random.fold_in(key, 7), -5.0, 5.0, (D, KV_HEADS * HEAD_DIM), jnp.float32) / math.sqrt(D)


def draw_w_key(key, part):
    return key_base(key).astype(jnp.bfloat16)


def draw_w_query(key, part):
    key = jax.random.fold_in(key, 3)
    own = jax.random.truncated_normal(key, -5.0, 5.0, (D, HEADS * HEAD_DIM), jnp.float32) / math.sqrt(D)
    return own.astype(jnp.bfloat16)


def draw_inputs(key, part):
    key = jax.random.fold_in(key, 5)
    shape = (SEQS, LEN, D)
    value = jax.random.truncated_normal(key, -6.0, 6.0, shape, jnp.float32)
    return value.astype(jnp.bfloat16)


def level_of(rng, extent, cuts, least, top_value):
    def one(axis_at, parts):
        steps = jax.random.uniform(jax.random.fold_in(jax.random.fold_in(rng, 6), axis_at), (parts,), jnp.float32, least / len(cuts), top_value / len(cuts))
        return jnp.repeat(jnp.exp(steps), extent[axis_at] // parts).reshape((-1,) + (1,) * (len(extent) - axis_at - 1))

    level = one(*cuts[0])
    for cut in cuts[1:]:
        level = level * one(*cut)
    return level


def scatter_about(key, extent, scale, reach, cuts=(), kind=jnp.bfloat16):
    result = scale * jax.random.normal(key, extent, jnp.float32)
    if cuts:
        result = result * level_of(key, extent, cuts, -0.22, 0.18)
    return jnp.clip(result, -reach, reach).astype(kind)


def setup_inputs(seed: int = 0) -> dict:
    arg_keys = jax.random.split(jax.random.key(seed), 6)
    inputs = draw_inputs(jax.random.fold_in(arg_keys[5], 71), 0)
    w_query = draw_w_query(jax.random.fold_in(arg_keys[5], 71), 0)
    w_key = draw_w_key(jax.random.fold_in(arg_keys[5], 71), 0)
    w_value = scatter_about(arg_keys[3], (D, KV_HEADS * HEAD_DIM), D ** -0.5, 0.09375, ((0, 16), (1, 4)))
    grad_out = scatter_about(arg_keys[4], (SEQS, LEN, HEADS * HEAD_DIM), 4.0, 24.0, ((0, 4), (1, 16), (2, 4)))
    return dict(inputs=inputs, w_query=w_query, w_key=w_key, w_value=w_value, grad_out=grad_out)


def attend_group(packed):
    query_grp, key_grp, value_grp, cot_grp = packed
    score_scale = HEAD_DIM ** -0.5
    length = key_grp.shape[0]
    position = jnp.arange(length, dtype=jnp.int32)
    causal = position[None, :] <= position[:, None]
    scores = jnp.einsum('gqd,kd->gqk', query_grp.astype(jnp.float32), key_grp.astype(jnp.float32)) * score_scale
    scores = jnp.where(causal, scores, -1e30)
    highest = jnp.max(scores, -1, keepdims=True)
    weights = jnp.exp(scores - highest)
    probs = weights / jnp.sum(weights, -1, keepdims=True)
    probs_low = probs.astype(jnp.bfloat16)
    attended = jnp.einsum('gqk,kd->gqd', probs_low.astype(jnp.float32), value_grp.astype(jnp.float32))
    delta = jnp.sum(cot_grp.astype(jnp.float32) * attended, -1, keepdims=True)
    grad_probs = jnp.einsum('gqd,kd->gqk', cot_grp.astype(jnp.float32), value_grp.astype(jnp.float32))
    grad_scores = (probs * (grad_probs - delta)).astype(jnp.bfloat16)
    grad_q = jnp.einsum('gqk,kd->gqd', grad_scores.astype(jnp.float32), key_grp.astype(jnp.float32)) * score_scale
    grad_k = jnp.einsum('gqk,gqd->kd', grad_scores.astype(jnp.float32), query_grp.astype(jnp.float32)) * score_scale
    grad_v = jnp.einsum('gqk,gqd->kd', probs_low.astype(jnp.float32), cot_grp.astype(jnp.float32))
    return grad_q.astype(jnp.bfloat16), grad_k.astype(jnp.bfloat16), grad_v.astype(jnp.bfloat16)


def reference(inputs, w_query, w_key, w_value, grad_out):
    group_size = HEADS // KV_HEADS

    def one_sequence(carry, pieces):
        tokens, cotangent = pieces
        queries = jnp.dot(tokens, w_query, preferred_element_type=jnp.float32).astype(jnp.bfloat16)
        keys = jnp.dot(tokens, w_key, preferred_element_type=jnp.float32).astype(jnp.bfloat16)
        values = jnp.dot(tokens, w_value, preferred_element_type=jnp.float32).astype(jnp.bfloat16)
        query_heads = queries.reshape(LEN, KV_HEADS, group_size, HEAD_DIM).transpose(1, 2, 0, 3)
        key_heads = keys.reshape(LEN, KV_HEADS, HEAD_DIM).transpose(1, 0, 2)
        value_heads = values.reshape(LEN, KV_HEADS, HEAD_DIM).transpose(1, 0, 2)
        cot_heads = cotangent.reshape(LEN, KV_HEADS, group_size, HEAD_DIM).transpose(1, 2, 0, 3)
        grad_q, grad_k, grad_v = lax.map(attend_group, (query_heads, key_heads, value_heads, cot_heads))
        grad_q = grad_q.transpose(2, 0, 1, 3).reshape(LEN, HEADS * HEAD_DIM)
        grad_k = grad_k.transpose(1, 0, 2).reshape(LEN, KV_HEADS * HEAD_DIM)
        grad_v = grad_v.transpose(1, 0, 2).reshape(LEN, KV_HEADS * HEAD_DIM)
        grad_tokens = jnp.dot(grad_q, w_query.T, preferred_element_type=jnp.float32)
        grad_tokens = grad_tokens + jnp.dot(grad_k, w_key.T, preferred_element_type=jnp.float32)
        grad_tokens = grad_tokens + jnp.dot(grad_v, w_value.T, preferred_element_type=jnp.float32)
        sum_query, sum_key, sum_value = carry
        sum_query = sum_query + jnp.dot(tokens.T, grad_q, preferred_element_type=jnp.float32)
        sum_key = sum_key + jnp.dot(tokens.T, grad_k, preferred_element_type=jnp.float32)
        sum_value = sum_value + jnp.dot(tokens.T, grad_v, preferred_element_type=jnp.float32)
        return (sum_query, sum_key, sum_value), grad_tokens.astype(jnp.bfloat16)

    start_sums = (jnp.zeros((D, HEADS * HEAD_DIM), jnp.float32),
                  jnp.zeros((D, KV_HEADS * HEAD_DIM), jnp.float32),
                  jnp.zeros((D, KV_HEADS * HEAD_DIM), jnp.float32))
    sums, grad_inputs = lax.scan(one_sequence, start_sums, (inputs, grad_out))
    return grad_inputs, sums[0], sums[1], sums[2]
```

```python
import functools

import jax
import jax.numpy as jnp
from jax import lax
from jax.experimental import pallas as pl
from jax.experimental.pallas import tpu as pltpu
from jax.sharding import PartitionSpec as P

HEAD_DIM = 128
ROWS, COLS, DEPTHS = 16, 4, 4
RING = ROWS // 2
TOK = 256
SEQ_TOK = 128
GROUP = 4
QW = 512
WIDTH = 768
KVW = 256
DCOL = 1024
TILE = 256
BF16, F32 = jnp.bfloat16, jnp.float32
SCALE = HEAD_DIM ** -0.5
EXP_SCALE = SCALE * 1.4426950408889634
NT = (((1,), (1,)), ((), ()))


class Net:
    def __init__(self, ssem, rsem):
        self.r = lax.axis_index("row")
        self.c = lax.axis_index("col")
        self.d = lax.axis_index("depth")
        self.z = self.r // 2
        self.core = lax.rem(self.r, 2)
        self.ssem, self.rsem = ssem, rsem
        self.count = 0
        self.sent = []
        self.peers = {
            "zr": {"row": lax.rem(self.r + 2, ROWS)},
            "zl": {"row": lax.rem(self.r + ROWS - 2, ROWS)},
            "sib": {"row": self.r + 1 - 2 * self.core},
            "yr": {"col": lax.rem(self.c + 1, COLS)},
            "yl": {"col": lax.rem(self.c + COLS - 1, COLS)},
            "xr": {"depth": lax.rem(self.d + 1, DEPTHS)},
            "xl": {"depth": lax.rem(self.d + DEPTHS - 1, DEPTHS)},
        }

    def barrier(self, names):
        bar = pltpu.get_barrier_semaphore()
        for name in names:
            pl.semaphore_signal(
                bar, inc=1, device_id=self.peers[name], device_id_type=pl.DeviceIdType.MESH
            )
        pl.semaphore_wait(bar, len(names))

    def send(self, src, dst, name):
        i = self.count
        self.count += 1
        copy = pltpu.make_async_remote_copy(
            src_ref=src,
            dst_ref=dst,
            send_sem=self.ssem.at[i],
            recv_sem=self.rsem.at[i],
            device_id=self.peers[name],
            device_id_type=pl.DeviceIdType.MESH,
        )
        copy.start()
        self.sent.append(copy)
        return copy

    def finish(self):
        for copy in self.sent:
            copy.wait_send()

    def zk(self, k):
        return lax.rem(self.z + k % RING, RING)


def ring_gather(net, slot, part_a, part_b, arrived):
    pend = {}
    pend["ra", 0] = net.send(slot(net.z, part_a), slot(net.z, part_a), "zr")
    pend["lb", 0] = net.send(slot(net.z, part_b), slot(net.z, part_b), "zl")
    pend["rb", 0] = net.send(slot(net.z, part_b), slot(net.z, part_b), "zr")
    pend["la", 0] = net.send(slot(net.z, part_a), slot(net.z, part_a), "zl")

    def step(s):
        for key, far in (("ra", 4), ("lb", 4), ("rb", 3), ("la", 3)):
            if s >= far:
                continue
            pend[key, s].wait_recv()
            k = -(s + 1) if key[0] == "r" else s + 1
            part = part_a if key[1] == "a" else part_b
            ref = slot(net.zk(k), part)
            if s + 1 < far:
                pend[key, s + 1] = net.send(ref, ref, "zr" if key[0] == "r" else "zl")
            arrived(s, k, key[1], ref)

    return step


def project_kernel(
    x_ref, wq_ref, wk_ref, wv_ref, qkv_ref, xt_out, wf_out, xf, wf, xt, ssem, rsem, lsem
):
    net = Net(ssem, rsem)
    c, d, core = net.c, net.d, net.core
    net.barrier(["zr", "zl", "sib", "yr", "yl", "xr", "xl"])

    own = wf.at[net.z, core]
    own[:, :, 0:QW] = wq_ref[...].reshape(4, 64, QW)
    own[:, :, QW : QW + 128] = wk_ref[...].reshape(4, 64, 128)
    own[:, :, QW + 128 :] = wv_ref[...].reshape(4, 64, 128)

    part_a, part_b = d, lax.rem(d + 1, DEPTHS)

    def slot(z, q):
        return wf.at[z, core, q]

    sib, cross = [], {}

    def arrived(s, k, half, ref):
        if half == "a":
            cross[k, "a"] = net.send(ref, ref, "xr")
        else:
            cross[k, "b"] = net.send(ref, ref, "xl")
        sib.append(net.send(ref, ref, "sib"))

    def crossed(s):
        for k in (-(s + 1), s + 1):
            for half in ("a", "b"):
                if s == 3 and (k > 0) != (half == "b"):
                    continue
                cross[k, half].wait_recv()
                q = lax.rem(d + (3 if half == "a" else 2), DEPTHS)
                ref = wf.at[net.zk(k), core, q]
                sib.append(net.send(ref, ref, "sib"))

    step = ring_gather(net, slot, part_a, part_b, arrived)
    ya_r = net.send(x_ref.at[0], xf.at[c, 0], "yr")
    yb_l = net.send(x_ref.at[1], xf.at[c, 1], "yl")
    yb_r = net.send(x_ref.at[1], xf.at[c, 1], "yr")
    ya_l = net.send(x_ref.at[0], xf.at[c, 0], "yl")
    sib.append(net.send(own, own, "sib"))
    xf[c] = x_ref[...]

    left, right = lax.rem(c + 3, COLS), lax.rem(c + 1, COLS)
    far = lax.rem(c + 2, COLS)

    def transpose(cc):
        for s in range(2):
            for k in range(DCOL // 128):
                xt[cc, k * 128 : (k + 1) * 128, s * 128 : (s + 1) * 128] = xf[
                    cc, s, :, k * 128 : (k + 1) * 128
                ].T

    step(0)
    transpose(c)
    step(1)
    ya_r.wait_recv()
    y2a = net.send(xf.at[left, 0], xf.at[left, 0], "yr")
    yb_l.wait_recv()
    y2b = net.send(xf.at[right, 1], xf.at[right, 1], "yl")
    crossed(0)
    step(2)
    crossed(1)
    yb_r.wait_recv()
    ya_l.wait_recv()
    step(3)
    crossed(2)
    transpose(left)
    transpose(right)
    crossed(3)
    y2a.wait_recv()
    y2b.wait_recv()
    transpose(far)
    for copy in sib:
        copy.wait_recv()
    out_x = pltpu.make_async_copy(xt, xt_out, lsem.at[0])
    out_w = pltpu.make_async_copy(wf, wf_out, lsem.at[1])
    out_x.start()
    out_w.start()
    acc = jnp.zeros((TOK, WIDTH), F32)
    for cc in range(COLS):
        acc = acc + jnp.dot(
            xf[cc].reshape(TOK, DCOL),
            wf[2 * cc : 2 * cc + 2].reshape(DCOL, WIDTH),
            preferred_element_type=F32,
        )
    qkv_ref[...] = acc.astype(BF16)
    net.finish()
    out_x.wait()
    out_w.wait()


def project(x, wq, wk, wv):
    vm = pl.BlockSpec(memory_space=pltpu.VMEM)
    hbm = pl.BlockSpec(memory_space=pl.ANY)
    n = 80
    return pl.pallas_call(
        project_kernel,
        name="project",
        out_shape=(
            jax.ShapeDtypeStruct((TOK, WIDTH), BF16),
            jax.ShapeDtypeStruct((COLS, DCOL, TOK), BF16),
            jax.ShapeDtypeStruct((RING, 2, 4, 64, WIDTH), BF16),
        ),
        in_specs=[vm] * 4,
        out_specs=(vm, hbm, hbm),
        scratch_shapes=[
            pltpu.VMEM((COLS, 2, SEQ_TOK, DCOL), BF16),
            pltpu.VMEM((RING, 2, 4, 64, WIDTH), BF16),
            pltpu.VMEM((COLS, DCOL, TOK), BF16),
            pltpu.SemaphoreType.DMA((n,)),
            pltpu.SemaphoreType.DMA((n,)),
            pltpu.SemaphoreType.DMA((2,)),
        ],
        compiler_params=pltpu.CompilerParams(
            collective_id=0, has_side_effects=True, vmem_limit_bytes=40 << 20
        ),
    )(x, wq, wk, wv)


def attend_kernel(
    qkv_ref, go_ref, rows_ref, kvb, qh, oh, prob, gprob, mblk, stat, dqt, part, fromsib, rin,
    ssem, rsem,
):
    net = Net(ssem, rsem)
    z, core, r = net.z, net.core, net.r
    for s in range(2):
        kvb[z, s, core] = qkv_ref[s * 128 : (s + 1) * 128, QW:]
        for h in range(GROUP):
            qh[s, h * 128 : (h + 1) * 128] = qkv_ref[
                s * 128 : (s + 1) * 128, h * 128 : (h + 1) * 128
            ]
            oh[s, h * 128 : (h + 1) * 128] = go_ref[s, :, h * 128 : (h + 1) * 128]
    net.barrier(["zr", "zl", "sib"])

    def slot(zz, half):
        return kvb.at[zz, half, core]

    sib = {}

    def arrived(s, k, half, ref):
        sib[k % RING, half] = net.send(ref, ref, "sib")

    sib[0, "a"] = net.send(slot(z, 0), slot(z, 0), "sib")
    sib[0, "b"] = net.send(slot(z, 1), slot(z, 1), "sib")
    step = ring_gather(net, slot, 0, 1, arrived)

    def scores(s, zz):
        kv = kvb[zz, s].reshape(2 * SEQ_TOK, KVW)
        st = lax.dot_general(kv[:, :HEAD_DIM], qh[s], NT, preferred_element_type=F32)
        dp = lax.dot_general(kv[:, HEAD_DIM:], oh[s], NT, preferred_element_type=F32)
        return st * EXP_SCALE, dp

    def first(s, carry):
        st, dp = scores(s, z)
        key = lax.broadcasted_iota(jnp.int32, (2 * SEQ_TOK, QW), 0)
        query = lax.rem(lax.broadcasted_iota(jnp.int32, (2 * SEQ_TOK, QW), 1), SEQ_TOK)
        st = jnp.where(key <= query + core * SEQ_TOK, st, -1e30)
        m = jnp.max(st, 0, keepdims=True)
        p = jnp.exp2(st - m)
        prob[z, s] = p
        gprob[z, s] = dp
        mblk[z, s] = m
        stat[s, 0:1] = m
        stat[s, 1:2] = jnp.sum(p, 0, keepdims=True)
        stat[s, 2:3] = jnp.sum(p * dp, 0, keepdims=True)
        return carry

    def more(zz):
        def one(s, carry):
            st, dp = scores(s, zz)
            old = stat[s, 0:1]
            m = jnp.maximum(old, jnp.max(st, 0, keepdims=True))
            p = jnp.exp2(st - m)
            fade = jnp.exp2(old - m)
            prob[zz, s] = p
            gprob[zz, s] = dp
            mblk[zz, s] = m
            stat[s, 0:1] = m
            stat[s, 1:2] = stat[s, 1:2] * fade + jnp.sum(p, 0, keepdims=True)
            stat[s, 2:3] = stat[s, 2:3] * fade + jnp.sum(p * dp, 0, keepdims=True)
            return carry

        @pl.when(zz < z)
        def _():
            lax.fori_loop(0, 2, one, 0)

    sib[0, "a"].wait_recv()
    sib[0, "b"].wait_recv()
    lax.fori_loop(0, 2, first, 0)
    part[...] = jnp.zeros_like(part)
    for s in range(4):
        step(s)
        for k in (-(s + 1), s + 1) if s < 3 else (4,):
            for half in ("a", "b"):
                sib[k % RING, half].wait_recv()
            more(net.zk(k))

    dqt[...] = jnp.zeros_like(dqt)
    for s in range(2):
        inv = 1.0 / stat[s, 1:2]
        stat[s, 3:4] = inv
        stat[s, 4:5] = stat[s, 2:3] * inv

    def back(zz, carry):
        for s in range(2):
            fac = jnp.exp2(mblk[zz, s] - stat[s, 0:1]) * stat[s, 3:4]
            p = prob[zz, s] * fac
            low = p.astype(BF16)
            ds = (p * (gprob[zz, s] - stat[s, 4:5])).astype(BF16)
            dv = jnp.dot(low, oh[s], preferred_element_type=F32)
            dk = jnp.dot(ds, qh[s], preferred_element_type=F32) * SCALE
            keys = kvb[zz, s].reshape(2 * SEQ_TOK, KVW)[:, :HEAD_DIM]
            dqt[s] += jnp.dot(keys.T, ds, preferred_element_type=F32)
            for co in range(2):
                part[zz, co, s, :, :HEAD_DIM] = dk[co * 128 : (co + 1) * 128].astype(BF16)
                part[zz, co, s, :, HEAD_DIM:] = dv[co * 128 : (co + 1) * 128].astype(BF16)
        return carry

    lax.fori_loop(0, z + 1, back, 0)

    def mine(zz, s):
        return part.at[zz, core, s]

    def fold(zz):
        part[zz, core] = (part[zz, core].astype(F32) + fromsib[zz].astype(F32)).astype(BF16)

    order = (4, 3, -3, 2, -2, 1, -1, 0)
    swap = {k: net.send(part.at[net.zk(k), 1 - core], fromsib.at[net.zk(k)], "sib") for k in order}
    for s in range(2):
        for h in range(GROUP):
            rows_ref[s * 128 : (s + 1) * 128, h * 128 : (h + 1) * 128] = (
                (dqt[s, :, h * 128 : (h + 1) * 128] * SCALE).T.astype(BF16)
            )
    got = {}

    def out(way, half, n):
        k = n if way == "r" else -n
        got[way, half, n] = net.send(
            mine(net.zk(k), half),
            rin.at[0 if way == "r" else 1, half, n - 1],
            "zr" if way == "r" else "zl",
        )

    def add(way, half, n, k):
        got[way, half, n].wait_recv()
        ref = mine(net.zk(k), half)
        src = rin.at[0 if way == "r" else 1, half, n - 1]
        ref[...] = (ref[...].astype(F32) + src[...].astype(F32)).astype(BF16)

    swap[4].wait_recv()
    fold(net.zk(4))
    out("r", 0, 4)
    out("l", 1, 4)
    for k in (3, -3):
        swap[k].wait_recv()
        fold(net.zk(k))
    out("r", 1, 3)
    out("l", 0, 3)
    add("r", 0, 4, 3)
    out("r", 0, 3)
    add("l", 1, 4, -3)
    out("l", 1, 3)
    for n in (2, 1):
        for k in (n, -n):
            swap[k].wait_recv()
            fold(net.zk(k))
        for way, half in (("r", 1), ("l", 0), ("r", 0), ("l", 1)):
            add(way, half, n + 1, n if way == "r" else -n)
            out(way, half, n)
    swap[0].wait_recv()
    for half in range(2):
        total = part[z, core, half].astype(F32) + fromsib[z, half].astype(F32)
        for way in ("r", "l"):
            got[way, half, 1].wait_recv()
        total = total + rin[0, half, 0].astype(F32) + rin[1, half, 0].astype(F32)
        rows_ref[half * 128 : (half + 1) * 128, QW:] = total.astype(BF16)
    net.finish()


def attend(qkv, go):
    vm = pl.BlockSpec(memory_space=pltpu.VMEM)
    n = 56
    return pl.pallas_call(
        attend_kernel,
        name="attend",
        out_shape=jax.ShapeDtypeStruct((TOK, WIDTH), BF16),
        in_specs=[vm] * 2,
        out_specs=vm,
        scratch_shapes=[
            pltpu.VMEM((RING, 2, 2, SEQ_TOK, KVW), BF16),
            pltpu.VMEM((2, QW, HEAD_DIM), BF16),
            pltpu.VMEM((2, QW, HEAD_DIM), BF16),
            pltpu.VMEM((RING, 2, 2 * SEQ_TOK, QW), F32),
            pltpu.VMEM((RING, 2, 2 * SEQ_TOK, QW), F32),
            pltpu.VMEM((RING, 2, 1, QW), F32),
            pltpu.VMEM((2, 8, QW), F32),
            pltpu.VMEM((2, HEAD_DIM, QW), F32),
            pltpu.VMEM((RING, 2, 2, SEQ_TOK, KVW), BF16),
            pltpu.VMEM((RING, 2, SEQ_TOK, KVW), BF16),
            pltpu.VMEM((2, 2, 4, SEQ_TOK, KVW), BF16),
            pltpu.SemaphoreType.DMA((n,)),
            pltpu.SemaphoreType.DMA((n,)),
        ],
        compiler_params=pltpu.CompilerParams(
            collective_id=1, has_side_effects=True, vmem_limit_bytes=48 << 20
        ),
    )(qkv, go)


def grads_kernel(
    rows_ref, xt_hbm, wf_hbm, gi_ref, gw_ref, wf, xt, gi, yin, dw, dwsib, xin, zin, fin,
    ssem, rsem, lsem,
):
    net = Net(ssem, rsem)
    z, core, c, d = net.z, net.core, net.c, net.d
    in_w = pltpu.make_async_copy(wf_hbm, wf, lsem.at[0])
    in_x = pltpu.make_async_copy(xt_hbm, xt, lsem.at[1])
    in_w.start()
    in_x.start()
    net.barrier(["zr", "zl", "sib", "yr", "yl", "xr", "xl"])
    in_w.wait()

    def input_part(cc):
        w = wf[pl.ds(2 * cc, 2)].reshape(DCOL, WIDTH)
        return lax.dot_general(rows_ref[...], w, NT, preferred_element_type=F32)

    def input_store(cc):
        gi[cc] = input_part(cc).astype(BF16).reshape(2, SEQ_TOK, DCOL)

    far, right, left = lax.rem(c + 2, COLS), lax.rem(c + 1, COLS), lax.rem(c + 3, COLS)
    input_store(far)
    y0 = net.send(gi.at[far, 0], yin.at[0], "yr")
    y1 = net.send(gi.at[far, 1], yin.at[1], "yl")
    input_store(right)
    y2 = net.send(gi.at[right, 1], yin.at[2], "yr")
    input_store(left)
    y3 = net.send(gi.at[left, 0], yin.at[3], "yl")
    in_x.wait()

    swap = {}

    def tile(k):
        zz = net.zk(k)
        for co in range(2):
            rows = xt[zz // 2, pl.ds(pl.multiple_of(lax.rem(zz, 2) * 512 + co * 256, 256), 256)]
            part = jnp.dot(rows, rows_ref[...], preferred_element_type=F32)
            dw[zz, co] = part.astype(BF16).reshape(4, 64, WIDTH)
        swap[k] = net.send(dw.at[zz, 1 - core], dwsib.at[zz], "sib")

    def add(ref, src):
        ref[...] = (ref[...].astype(F32) + src[...].astype(F32)).astype(BF16)

    quarter_a, quarter_b = d, lax.rem(d + 1, DEPTHS)
    cross = {}

    def fold(k):
        zz = net.zk(k)
        swap[k].wait_recv()
        add(dw.at[zz, core], dwsib.at[zz])
        ql, qr = lax.rem(d + 3, DEPTHS), lax.rem(d + 2, DEPTHS)
        cross[k, "a"] = net.send(dw.at[zz, core, ql], xin.at[zz, 0], "xl")
        cross[k, "b"] = net.send(dw.at[zz, core, qr], xin.at[zz, 1], "xr")

    def keep(k):
        zz = net.zk(k)
        cross[k, "a"].wait_recv()
        add(dw.at[zz, core, quarter_a], xin.at[zz, 0])
        cross[k, "b"].wait_recv()
        add(dw.at[zz, core, quarter_b], xin.at[zz, 1])

    got = {}

    def part_of(half):
        return quarter_a if half == 0 else quarter_b

    def out(way, half, n):
        k = n if way == "r" else -n
        got[way, half, n] = net.send(
            dw.at[net.zk(k), core, part_of(half)],
            zin.at[0 if way == "r" else 1, half, n - 1],
            "zr" if way == "r" else "zl",
        )

    def take(way, half, n, k):
        got[way, half, n].wait_recv()
        add(dw.at[net.zk(k), core, part_of(half)], zin.at[0 if way == "r" else 1, half, n - 1])

    tile(4)
    tile(3)
    tile(-3)
    fold(4)
    tile(2)
    tile(-2)
    fold(3)
    fold(-3)
    tile(1)
    tile(-1)
    keep(4)
    out("r", 0, 4)
    out("l", 1, 4)
    tile(0)
    fold(2)
    fold(-2)
    fold(1)
    fold(-1)
    fold(0)
    keep(3)
    out("r", 1, 3)
    keep(-3)
    out("l", 0, 3)
    y0.wait_recv()
    add(gi.at[right, 0], yin.at[0])
    y4 = net.send(gi.at[right, 0], yin.at[4], "yr")
    y1.wait_recv()
    add(gi.at[left, 1], yin.at[1])
    y5 = net.send(gi.at[left, 1], yin.at[5], "yl")
    take("r", 0, 4, 3)
    out("r", 0, 3)
    take("l", 1, 4, -3)
    out("l", 1, 3)
    own = input_part(c)
    for n in (2, 1):
        keep(n)
        keep(-n)
        for way, half in (("r", 1), ("l", 0), ("r", 0), ("l", 1)):
            take(way, half, n + 1, n if way == "r" else -n)
            out(way, half, n)
    keep(0)
    take("r", 1, 1, 0)
    take("l", 1, 1, 0)
    last = net.send(dw.at[z, core, quarter_b], fin, "xr")
    take("r", 0, 1, 0)
    take("l", 0, 1, 0)
    for copy in (y2, y3, y4, y5):
        copy.wait_recv()
    gi_ref[0] = (own[:SEQ_TOK] + yin[3].astype(F32) + yin[4].astype(F32)).astype(BF16)
    gi_ref[1] = (own[SEQ_TOK:] + yin[2].astype(F32) + yin[5].astype(F32)).astype(BF16)
    last.wait_recv()
    gw_ref[...] = dw[z, core, quarter_a].astype(F32) + fin[...].astype(F32)
    net.finish()


def grads(rows, xt, wf):
    vm = pl.BlockSpec(memory_space=pltpu.VMEM)
    hbm = pl.BlockSpec(memory_space=pl.ANY)
    n = 64
    return pl.pallas_call(
        grads_kernel,
        name="grads",
        out_shape=(
            jax.ShapeDtypeStruct((2, SEQ_TOK, DCOL), BF16),
            jax.ShapeDtypeStruct((64, WIDTH), F32),
        ),
        in_specs=[vm, hbm, hbm],
        out_specs=(vm, vm),
        scratch_shapes=[
            pltpu.VMEM((RING, 2, 4, 64, WIDTH), BF16),
            pltpu.VMEM((COLS, DCOL, TOK), BF16),
            pltpu.VMEM((COLS, 2, SEQ_TOK, DCOL), BF16),
            pltpu.VMEM((6, SEQ_TOK, DCOL), BF16),
            pltpu.VMEM((RING, 2, 4, 64, WIDTH), BF16),
            pltpu.VMEM((RING, 4, 64, WIDTH), BF16),
            pltpu.VMEM((RING, 2, 64, WIDTH), BF16),
            pltpu.VMEM((2, 2, 4, 64, WIDTH), BF16),
            pltpu.VMEM((64, WIDTH), BF16),
            pltpu.SemaphoreType.DMA((n,)),
            pltpu.SemaphoreType.DMA((n,)),
            pltpu.SemaphoreType.DMA((2,)),
        ],
        compiler_params=pltpu.CompilerParams(
            collective_id=2, has_side_effects=True, vmem_limit_bytes=48 << 20
        ),
    )(rows, xt, wf)


def body(inputs, w_query, w_key, w_value, grad_out):
    qkv, xt, wf = project(inputs, w_query, w_key, w_value)
    rows = attend(qkv, grad_out)
    grad_inputs, gw = grads(rows, xt, wf)
    return grad_inputs, gw[:, :QW], gw[:, QW : QW + 128], gw[:, QW + 128 :]


def solution(mesh):
    return jax.shard_map(
        body,
        mesh=mesh,
        in_specs=(
            P("depth", "row", "col"),
            P("row", "col"),
            P("row", "col"),
            P("row", "col"),
            P("depth", "row", "col"),
        ),
        out_specs=(
            P("depth", "row", "col"),
            P(("row", "depth"), "col"),
            P(("row", "depth"), "col"),
            P(("row", "depth"), "col"),
        ),
        check_vma=False,
    )
```

```python
import functools

import jax
import jax.numpy as jnp
from jax import lax
from jax.experimental import pallas as pl
from jax.experimental.pallas import tpu as pltpu
from jax.sharding import PartitionSpec as P

HEAD_DIM = 128
ROWS, COLS, DEPTHS = 16, 4, 4
RING = ROWS // 2
TOK = 256
SEQ_TOK = 128
GROUP = 4
QW = 512
WIDTH = 768
KVW = 256
COPIES = 272
DCOL = 1024
TILE = 256
BF16, F32 = jnp.bfloat16, jnp.float32
SCALE = HEAD_DIM ** -0.5
EXP_SCALE = SCALE * 1.4426950408889634
NT = (((1,), (1,)), ((), ()))


class Net:
    def __init__(self, ssem, rsem):
        self.r = lax.axis_index("row")
        self.c = lax.axis_index("col")
        self.d = lax.axis_index("depth")
        self.z = self.r // 2
        self.core = lax.rem(self.r, 2)
        self.ssem, self.rsem = ssem, rsem
        self.count = 0
        self.sent = []
        self.peers = {
            "zr": {"row": lax.rem(self.r + 2, ROWS)},
            "zl": {"row": lax.rem(self.r + ROWS - 2, ROWS)},
            "sib": {"row": self.r + 1 - 2 * self.core},
            "yr": {"col": lax.rem(self.c + 1, COLS)},
            "yl": {"col": lax.rem(self.c + COLS - 1, COLS)},
            "yf": {"col": lax.rem(self.c + 2, COLS)},
            "xr": {"depth": lax.rem(self.d + 1, DEPTHS)},
            "xl": {"depth": lax.rem(self.d + DEPTHS - 1, DEPTHS)},
        }

    def barrier(self, names):
        bar = pltpu.get_barrier_semaphore()
        for name in names:
            pl.semaphore_signal(
                bar, inc=1, device_id=self.peers[name], device_id_type=pl.DeviceIdType.MESH
            )
        pl.semaphore_wait(bar, len(names))

    def send(self, src, dst, name):
        i = self.count
        self.count += 1
        copy = pltpu.make_async_remote_copy(
            src_ref=src,
            dst_ref=dst,
            send_sem=self.ssem.at[i],
            recv_sem=self.rsem.at[i],
            device_id=self.peers[name],
            device_id_type=pl.DeviceIdType.MESH,
        )
        copy.start()
        self.sent.append(copy)
        return copy

    def release(self, copies):
        for copy in copies:
            copy.wait_send()
        self.sent = [one for one in self.sent if all(one is not copy for copy in copies)]

    def finish(self):
        for copy in self.sent:
            copy.wait_send()

    def zk(self, k):
        return lax.rem(self.z + k % RING, RING)


def ring_gather(net, slot, part_a, part_b, arrived):
    pend = {}
    pend["ra", 0] = net.send(slot(net.z, part_a), slot(net.z, part_a), "zr")
    pend["lb", 0] = net.send(slot(net.z, part_b), slot(net.z, part_b), "zl")
    pend["rb", 0] = net.send(slot(net.z, part_b), slot(net.z, part_b), "zr")
    pend["la", 0] = net.send(slot(net.z, part_a), slot(net.z, part_a), "zl")

    def step(s):
        for key, far in (("ra", 4), ("lb", 4), ("rb", 3), ("la", 3)):
            if s >= far:
                continue
            pend[key, s].wait_recv()
            k = -(s + 1) if key[0] == "r" else s + 1
            part = part_a if key[1] == "a" else part_b
            ref = slot(net.zk(k), part)
            if s + 1 < far:
                pend[key, s + 1] = net.send(ref, ref, "zr" if key[0] == "r" else "zl")
            arrived(s, k, key[1], ref)

    return step


class WeightSum:
    def __init__(self, net, width, xt, rows, dw, dwsib, xin, zin, fin):
        self.net, self.width, self.xt, self.rows = net, width, xt, rows
        self.dw, self.dwsib, self.xin, self.zin, self.fin = dw, dwsib, xin, zin, fin
        self.quarter = (net.d, lax.rem(net.d + 1, DEPTHS))
        self.swap, self.cross, self.got = {}, {}, {}

    def tile(self, k):
        net, zz = self.net, self.net.zk(k)
        start = pl.multiple_of(lax.rem(zz, 2) * 512, 512)
        rows = self.xt[zz // 2, pl.ds(start, 512)]
        part = jnp.dot(rows, self.rows[...], preferred_element_type=F32)
        self.dw[zz] = part.astype(BF16).reshape(2, 4, 64, self.width)
        self.swap[k] = net.send(self.dw.at[zz, 1 - net.core], self.dwsib.at[zz], "sib")

    def fold(self, k):
        net, zz = self.net, self.net.zk(k)
        self.swap[k].wait_recv()
        add(self.dw.at[zz, net.core], self.dwsib.at[zz])
        ql, qr = lax.rem(net.d + 3, DEPTHS), lax.rem(net.d + 2, DEPTHS)
        self.cross[k, 0] = net.send(self.dw.at[zz, net.core, ql], self.xin.at[zz, 0], "xl")
        self.cross[k, 1] = net.send(self.dw.at[zz, net.core, qr], self.xin.at[zz, 1], "xr")

    def keep(self, k):
        zz = self.net.zk(k)
        for half in range(2):
            self.cross[k, half].wait_recv()
            add(self.dw.at[zz, self.net.core, self.quarter[half]], self.xin.at[zz, half])

    def out(self, way, half, n):
        net = self.net
        zz = net.zk(n if way == "r" else -n)
        self.got[way, half, n] = net.send(
            self.dw.at[zz, net.core, self.quarter[half]],
            self.zin.at[0 if way == "r" else 1, half, n - 1],
            "zr" if way == "r" else "zl",
        )

    def take(self, way, half, n):
        net = self.net
        self.got[way, half, n].wait_recv()
        zz = net.zk(n - 1 if way == "r" else 1 - n)
        add(
            self.dw.at[zz, net.core, self.quarter[half]],
            self.zin.at[0 if way == "r" else 1, half, n - 1],
        )

    def start(self):
        self.keep(4)
        self.out("r", 0, 4)
        self.out("l", 1, 4)

    def second(self):
        self.keep(3)
        self.out("r", 1, 3)
        self.keep(-3)
        self.out("l", 0, 3)

    def third(self):
        self.take("r", 0, 4)
        self.out("r", 0, 3)
        self.take("l", 1, 4)
        self.out("l", 1, 3)

    def later(self, n):
        self.keep(n)
        self.keep(-n)
        for way, half in (("r", 1), ("l", 0), ("r", 0), ("l", 1)):
            self.take(way, half, n + 1)
            self.out(way, half, n)

    def last(self):
        net = self.net
        self.keep(0)
        self.take("r", 1, 1)
        self.take("l", 1, 1)
        self.final = net.send(self.dw.at[net.z, net.core, self.quarter[1]], self.fin, "xr")
        self.take("r", 0, 1)
        self.take("l", 0, 1)

    def result(self):
        net = self.net
        self.final.wait_recv()
        return self.dw[net.z, net.core, self.quarter[0]].astype(F32) + self.fin[...].astype(F32)


def add(ref, src):
    ref[...] = (ref[...].astype(F32) + src[...].astype(F32)).astype(BF16)


def fused_kernel(
    x_hbm, wq_hbm, wk_hbm, wv_hbm, go_hbm, gi_ref, gq_ref, gk_ref, gv_ref,
    xf, wqf, wkf, xt, kvb, qh, oh, prob, gprob, mblk, stat, dqt, part, fromsib, rin,
    rq, rkv, wkv, yin, dwq, dwqsib, xqin, zqin, fqin, dwk, dwksib, xkin, zkin, fkin,
    ssem, rsem, lsem,
):
    net = Net(ssem, rsem)
    c, d, z, core = net.c, net.d, net.z, net.core
    left, right, far = lax.rem(c + 3, COLS), lax.rem(c + 1, COLS), lax.rem(c + 2, COLS)
    own_q, own_k = wqf.at[z, core], wkf.at[z, core]
    local = []

    def fetch(src, dst):
        copy = pltpu.make_async_copy(src, dst, lsem.at[len(local)])
        copy.start()
        local.append(copy)

    fetch(wk_hbm, own_k.at[:, :, pl.ds(0, 128)])
    fetch(wv_hbm, own_k.at[:, :, pl.ds(128, 128)])
    fetch(wq_hbm, own_q)
    fetch(x_hbm, xf.at[c])
    for s in range(2):
        for h in range(GROUP):
            fetch(go_hbm.at[s, :, pl.ds(h * 128, 128)], oh.at[s, pl.ds(h * 128, 128)])
    net.barrier(["zr", "zl", "sib", "yr", "yl", "yf", "xr", "xl"])
    for copy in local[:4]:
        copy.wait()

    class Spread:
        def __init__(self, full):
            self.full, self.sib, self.cross = full, [], {}
            own = full.at[z, core]
            self.step = ring_gather(
                net,
                lambda zz, q: full.at[zz, core, q],
                d,
                lax.rem(d + 1, DEPTHS),
                self.arrived,
            )
            self.sib.append(net.send(own, own, "sib"))

        def arrived(self, s, k, half, ref):
            self.cross[k, half] = net.send(ref, ref, "xr" if half == "a" else "xl")
            self.sib.append(net.send(ref, ref, "sib"))

        def crossed(self, s):
            for k in (-(s + 1), s + 1):
                for half in ("a", "b"):
                    if s == 3 and (k > 0) != (half == "b"):
                        continue
                    self.cross[k, half].wait_recv()
                    q = lax.rem(d + (3 if half == "a" else 2), DEPTHS)
                    ref = self.full.at[net.zk(k), core, q]
                    self.sib.append(net.send(ref, ref, "sib"))

        def complete(self):
            for copy in self.sib:
                copy.wait_recv()

    wk = Spread(wkf)
    ya_r = net.send(xf.at[c, 0], xf.at[c, 0], "yr")
    yb_l = net.send(xf.at[c, 1], xf.at[c, 1], "yl")
    yb_r = net.send(xf.at[c, 1], xf.at[c, 1], "yr")
    ya_l = net.send(xf.at[c, 0], xf.at[c, 0], "yl")
    wq = Spread(wqf)

    def transpose(cc):
        for s in range(2):
            for k in range(DCOL // 128):
                xt[cc, k * 128 : (k + 1) * 128, s * 128 : (s + 1) * 128] = xf[
                    cc, s, :, k * 128 : (k + 1) * 128
                ].T

    wk.step(0)
    transpose(c)
    wq.step(0)
    wk.step(1)
    wk.crossed(0)
    ya_r.wait_recv()
    y2a = net.send(xf.at[left, 0], xf.at[left, 0], "yr")
    yb_l.wait_recv()
    y2b = net.send(xf.at[right, 1], xf.at[right, 1], "yl")
    wq.step(1)
    wq.crossed(0)
    wk.step(2)
    wk.crossed(1)
    wq.step(2)
    wq.crossed(1)
    wk.step(3)
    wk.crossed(2)
    yb_r.wait_recv()
    ya_l.wait_recv()
    transpose(left)
    transpose(right)
    wq.step(3)
    wk.crossed(3)
    wq.crossed(2)
    wk.complete()

    def project(chunks, full, width):
        total = None
        for cc in chunks:
            w = full[pl.ds(2 * cc, 2)].reshape(DCOL, width)
            part = jnp.dot(xf[cc].reshape(TOK, DCOL), w, preferred_element_type=F32)
            total = part if total is None else total + part
        return total

    near = project((c, left, right), wkf, KVW)
    y2a.wait_recv()
    y2b.wait_recv()
    near = (near + project((far,), wkf, KVW)).astype(BF16)

    def slot(zz, half):
        return kvb.at[zz, half, core]

    kvb[z, 0, core] = near[:SEQ_TOK]
    kvb[z, 1, core] = near[SEQ_TOK:]
    kvsib = {}

    def kv_arrived(s, k, half, ref):
        kvsib[k % RING, half] = net.send(ref, ref, "sib")

    kvsib[0, "a"] = net.send(slot(z, 0), slot(z, 0), "sib")
    kvsib[0, "b"] = net.send(slot(z, 1), slot(z, 1), "sib")
    step = ring_gather(net, slot, 0, 1, kv_arrived)

    wkv_got = []
    for i, (cc, name) in enumerate(((far, "yf"), (right, "yr"), (left, "yl"))):
        wkv_got.append(net.send(wkf.at[pl.ds(2 * cc, 2), core], wkv.at[i, core], name))
    wq.crossed(3)
    step(0)
    wq.complete()
    query = project((c, left, right, far), wqf, QW).astype(BF16)
    for s in range(2):
        for h in range(GROUP):
            qh[s, h * 128 : (h + 1) * 128] = query[
                s * 128 : (s + 1) * 128, h * 128 : (h + 1) * 128
            ]
    for copy in local[4:]:
        copy.wait()
    transpose(far)
    net.release((ya_r, yb_l, yb_r, ya_l, y2a, y2b))

    def scores(s, zz):
        kv = kvb[zz, s].reshape(2 * SEQ_TOK, KVW)
        st = lax.dot_general(kv[:, :HEAD_DIM], qh[s], NT, preferred_element_type=F32)
        dp = lax.dot_general(kv[:, HEAD_DIM:], oh[s], NT, preferred_element_type=F32)
        return st * EXP_SCALE, dp

    def begin(s, carry):
        st, dp = scores(s, z)
        key = lax.broadcasted_iota(jnp.int32, (2 * SEQ_TOK, QW), 0)
        query_pos = lax.rem(lax.broadcasted_iota(jnp.int32, (2 * SEQ_TOK, QW), 1), SEQ_TOK)
        st = jnp.where(key <= query_pos + core * SEQ_TOK, st, -1e30)
        m = jnp.max(st, 0, keepdims=True)
        p = jnp.exp2(st - m)
        prob[z, s] = p
        gprob[z, s] = dp
        mblk[z, s] = m
        stat[s, 0:1] = m
        stat[s, 1:2] = jnp.sum(p, 0, keepdims=True)
        stat[s, 2:3] = jnp.sum(p * dp, 0, keepdims=True)
        return carry

    def more(zz):
        def one(s, carry):
            st, dp = scores(s, zz)
            old = stat[s, 0:1]
            m = jnp.maximum(old, jnp.max(st, 0, keepdims=True))
            p = jnp.exp2(st - m)
            fade = jnp.exp2(old - m)
            prob[zz, s] = p
            gprob[zz, s] = dp
            mblk[zz, s] = m
            stat[s, 0:1] = m
            stat[s, 1:2] = stat[s, 1:2] * fade + jnp.sum(p, 0, keepdims=True)
            stat[s, 2:3] = stat[s, 2:3] * fade + jnp.sum(p * dp, 0, keepdims=True)
            return carry

        @pl.when(zz < z)
        def _():
            lax.fori_loop(0, 2, one, 0)

    kvsib[0, "a"].wait_recv()
    kvsib[0, "b"].wait_recv()
    lax.fori_loop(0, 2, begin, 0)
    part[...] = jnp.zeros_like(part)
    dqt[...] = jnp.zeros_like(dqt)
    wkv_sib = []
    for s in range(4):
        if s:
            step(s)
        if s == 3:
            for i, copy in enumerate(wkv_got):
                copy.wait_recv()
                wkv_sib.append(net.send(wkv.at[i, core], wkv.at[i, core], "sib"))
        for k in (-(s + 1), s + 1) if s < 3 else (4,):
            for half in ("a", "b"):
                kvsib[k % RING, half].wait_recv()
            more(net.zk(k))

    for s in range(2):
        inv = 1.0 / stat[s, 1:2]
        stat[s, 3:4] = inv
        stat[s, 4:5] = stat[s, 2:3] * inv

    def back_block(zz):
        for s in range(2):
            fac = jnp.exp2(mblk[zz, s] - stat[s, 0:1]) * stat[s, 3:4]
            p = prob[zz, s] * fac
            low = p.astype(BF16)
            ds = (p * (gprob[zz, s] - stat[s, 4:5])).astype(BF16)
            dv = jnp.dot(low, oh[s], preferred_element_type=F32)
            dk = jnp.dot(ds, qh[s], preferred_element_type=F32) * SCALE
            keys = kvb[zz, s].reshape(2 * SEQ_TOK, KVW)[:, :HEAD_DIM]
            dqt[s] += jnp.dot(keys.T, ds, preferred_element_type=F32)
            for co in range(2):
                part[zz, co, s, :, :HEAD_DIM] = dk[co * 128 : (co + 1) * 128].astype(BF16)
                part[zz, co, s, :, HEAD_DIM:] = dv[co * 128 : (co + 1) * 128].astype(BF16)

    swap = {}

    def back(n):
        def one(i, carry):
            zz = lax.rem(z + n + i * (2 * RING - 2 * n), RING)

            @pl.when(zz <= z)
            def _():
                back_block(zz)

            return carry

        ks = (n, -n) if n % 4 else (n,)
        lax.fori_loop(0, len(ks), one, 0)
        for k in ks:
            swap[k] = net.send(part.at[net.zk(k), 1 - core], fromsib.at[net.zk(k)], "sib")

    def fold(k):
        swap[k].wait_recv()
        add(part.at[net.zk(k), core], fromsib.at[net.zk(k)])

    got = {}

    def out(way, half, n):
        got[way, half, n] = net.send(
            part.at[net.zk(n if way == "r" else -n), core, half],
            rin.at[0 if way == "r" else 1, half, n - 1],
            "zr" if way == "r" else "zl",
        )

    def take(way, half, n):
        got[way, half, n].wait_recv()
        add(
            part.at[net.zk(n - 1 if way == "r" else 1 - n), core, half],
            rin.at[0 if way == "r" else 1, half, n - 1],
        )

    def later(n):
        fold(n)
        fold(-n)
        for way, half in (("r", 1), ("l", 0), ("r", 0), ("l", 1)):
            take(way, half, n + 1)
            out(way, half, n)

    back(4)
    back(3)
    fold(4)
    out("r", 0, 4)
    out("l", 1, 4)
    back(2)
    fold(3)
    fold(-3)
    out("r", 1, 3)
    out("l", 0, 3)
    back(1)
    back(0)

    for s in range(2):
        for h in range(GROUP):
            rq[s * 128 : (s + 1) * 128, h * 128 : (h + 1) * 128] = (
                (dqt[s, :, h * 128 : (h + 1) * 128] * SCALE).T.astype(BF16)
            )

    def input_part(cc):
        w = wqf[pl.ds(2 * cc, 2)].reshape(DCOL, QW)
        return lax.dot_general(rq[...], w, NT, preferred_element_type=F32)

    def input_store(i, cc):
        xf[i] = input_part(cc).astype(BF16).reshape(2, SEQ_TOK, DCOL)

    to_far, to_right, to_left = xf.at[0], xf.at[1], xf.at[2]
    input_store(0, far)
    y0 = net.send(to_far.at[0], yin.at[0], "yr")
    y1 = net.send(to_far.at[1], yin.at[1], "yl")
    take("r", 0, 4)
    out("r", 0, 3)
    take("l", 1, 4)
    out("l", 1, 3)
    input_store(1, right)
    y2 = net.send(to_right.at[1], yin.at[2], "yr")
    input_store(2, left)
    y3 = net.send(to_left.at[0], yin.at[3], "yl")

    wsq = WeightSum(net, QW, xt, rq, dwq, dwqsib, xqin, zqin, fqin)
    wsk = WeightSum(net, KVW, xt, rkv.at[c], dwk, dwksib, xkin, zkin, fkin)
    for k in (4, 3, -3, 2, -2, 1, -1, 0):
        wsq.tile(k)
    for k in (4, 3, -3):
        wsq.fold(k)
    later(2)
    for k in (2, -2, 1, -1):
        wsq.fold(k)
    y0.wait_recv()
    add(to_right.at[0], yin.at[0])
    y4 = net.send(to_right.at[0], yin.at[4], "yr")
    y1.wait_recv()
    add(to_left.at[1], yin.at[1])
    y5 = net.send(to_left.at[1], yin.at[5], "yl")
    later(1)
    wsq.start()
    wsq.second()

    fold(0)
    for half in range(2):
        total = part[z, core, half].astype(F32)
        for way in range(2):
            got["rl"[way], half, 1].wait_recv()
            total = total + rin[way, half, 0].astype(F32)
        rkv[c, half * 128 : (half + 1) * 128] = total.astype(BF16)
    kv_sent = [net.send(rkv.at[c], rkv.at[c], name) for name in ("yf", "yr", "yl")]
    for k in (4, 3, -3, 2, -2, 1, -1, 0):
        wsk.tile(k)
    wsq.third()
    for k in (4, 3, -3, 2, -2, 1, -1):
        wsk.fold(k)
    wsq.fold(0)
    wsk.fold(0)
    total = input_part(c)
    wsq.later(2)
    wsk.start()
    wsk.second()
    wsq.later(1)
    wsk.third()
    wsk.later(2)
    wsq.last()
    wsk.later(1)
    for copy in wkv_sib:
        copy.wait_recv()

    def key_share(cc, w):
        return lax.dot_general(
            rkv[cc], w.reshape(DCOL, KVW), NT, preferred_element_type=F32
        )

    total = total + key_share(c, wkf[pl.ds(2 * c, 2)])
    for i, cc in enumerate((far, left, right)):
        kv_sent[i].wait_recv()
        w = jnp.stack([wkv[i, 0], wkv[i, 1]], 1)
        total = total + key_share(cc, w)
    wsk.last()
    for copy in (y2, y3, y4, y5):
        copy.wait_recv()
    gi_ref[0] = (total[:SEQ_TOK] + yin[3].astype(F32) + yin[4].astype(F32)).astype(BF16)
    gi_ref[1] = (total[SEQ_TOK:] + yin[2].astype(F32) + yin[5].astype(F32)).astype(BF16)
    gq_ref[...] = wsq.result()
    gkv = wsk.result()
    gk_ref[...] = gkv[:, :HEAD_DIM]
    gv_ref[...] = gkv[:, HEAD_DIM:]
    net.finish()
    assert net.count <= COPIES, net.count


def deliver_kernel(*refs):
    for src, dst in zip(refs[:4], refs[4:]):
        dst[...] = src[...]


def body(inputs, w_query, w_key, w_value, grad_out):
    vm = pl.BlockSpec(memory_space=pltpu.VMEM)
    hbm = pl.BlockSpec(memory_space=pltpu.HBM)
    results = pl.pallas_call(
        fused_kernel,
        name="fused",
        out_shape=(
            jax.ShapeDtypeStruct((2, SEQ_TOK, DCOL), BF16),
            jax.ShapeDtypeStruct((64, QW), F32),
            jax.ShapeDtypeStruct((64, HEAD_DIM), F32),
            jax.ShapeDtypeStruct((64, HEAD_DIM), F32),
        ),
        in_specs=[hbm] * 5,
        out_specs=(vm,) * 4,
        scratch_shapes=[
            pltpu.VMEM((COLS, 2, SEQ_TOK, DCOL), BF16),
            pltpu.VMEM((RING, 2, 4, 64, QW), BF16),
            pltpu.VMEM((RING, 2, 4, 64, KVW), BF16),
            pltpu.VMEM((COLS, DCOL, TOK), BF16),
            pltpu.VMEM((RING, 2, 2, SEQ_TOK, KVW), BF16),
            pltpu.VMEM((2, QW, HEAD_DIM), BF16),
            pltpu.VMEM((2, QW, HEAD_DIM), BF16),
            pltpu.VMEM((RING, 2, 2 * SEQ_TOK, QW), F32),
            pltpu.VMEM((RING, 2, 2 * SEQ_TOK, QW), F32),
            pltpu.VMEM((RING, 2, 1, QW), F32),
            pltpu.VMEM((2, 8, QW), F32),
            pltpu.VMEM((2, HEAD_DIM, QW), F32),
            pltpu.VMEM((RING, 2, 2, SEQ_TOK, KVW), BF16),
            pltpu.VMEM((RING, 2, SEQ_TOK, KVW), BF16),
            pltpu.VMEM((2, 2, 4, SEQ_TOK, KVW), BF16),
            pltpu.VMEM((TOK, QW), BF16),
            pltpu.VMEM((COLS, TOK, KVW), BF16),
            pltpu.VMEM((3, 2, 2, 4, 64, KVW), BF16),
            pltpu.VMEM((6, SEQ_TOK, DCOL), BF16),
            pltpu.VMEM((RING, 2, 4, 64, QW), BF16),
            pltpu.VMEM((RING, 4, 64, QW), BF16),
            pltpu.VMEM((RING, 2, 64, QW), BF16),
            pltpu.VMEM((2, 2, 4, 64, QW), BF16),
            pltpu.VMEM((64, QW), BF16),
            pltpu.VMEM((RING, 2, 4, 64, KVW), BF16),
            pltpu.VMEM((RING, 4, 64, KVW), BF16),
            pltpu.VMEM((RING, 2, 64, KVW), BF16),
            pltpu.VMEM((2, 2, 4, 64, KVW), BF16),
            pltpu.VMEM((64, KVW), BF16),
            pltpu.SemaphoreType.DMA((COPIES,)),
            pltpu.SemaphoreType.DMA((COPIES,)),
            pltpu.SemaphoreType.DMA((16,)),
        ],
        compiler_params=pltpu.CompilerParams(
            collective_id=0, has_side_effects=True, vmem_limit_bytes=58 << 20
        ),
    )(
        inputs,
        w_query.reshape(4, 64, QW),
        w_key.reshape(4, 64, HEAD_DIM),
        w_value.reshape(4, 64, HEAD_DIM),
        grad_out,
    )
    return pl.pallas_call(
        deliver_kernel,
        name="deliver",
        out_shape=[jax.ShapeDtypeStruct(one.shape, one.dtype) for one in results],
        in_specs=[vm] * 4,
        out_specs=[vm] * 4,
    )(*results)


def solution(mesh):
    return jax.shard_map(
        body,
        mesh=mesh,
        in_specs=(
            P("depth", "row", "col"),
            P("row", "col"),
            P("row", "col"),
            P("row", "col"),
            P("depth", "row", "col"),
        ),
        out_specs=(
            P("depth", "row", "col"),
            P(("row", "depth"), "col"),
            P(("row", "depth"), "col"),
            P(("row", "depth"), "col"),
        ),
        check_vma=False,
    )
```

```python
import functools

import jax
import jax.numpy as jnp
from jax import lax
from jax.experimental import pallas as pl
from jax.experimental.pallas import tpu as pltpu
from jax.sharding import PartitionSpec as P

HEAD_DIM = 128
ROWS, COLS, DEPTHS = 16, 4, 4
RING = ROWS // 2
TOK = 256
SEQ_TOK = 128
GROUP = 4
QW = 512
WIDTH = 768
KVW = 256
COPIES = 288
DCOL = 1024
TILE = 256
BF16, F32 = jnp.bfloat16, jnp.float32
SCALE = HEAD_DIM ** -0.5
EXP_SCALE = SCALE * 1.4426950408889634
NT = (((1,), (1,)), ((), ()))


class Net:
    def __init__(self, ssem, rsem):
        self.r = lax.axis_index("row")
        self.c = lax.axis_index("col")
        self.d = lax.axis_index("depth")
        self.z = self.r // 2
        self.core = lax.rem(self.r, 2)
        self.ssem, self.rsem = ssem, rsem
        self.count = 0
        self.sent = []
        self.peers = {
            "zr": {"row": lax.rem(self.r + 2, ROWS)},
            "zl": {"row": lax.rem(self.r + ROWS - 2, ROWS)},
            "sib": {"row": self.r + 1 - 2 * self.core},
            "yr": {"col": lax.rem(self.c + 1, COLS)},
            "yl": {"col": lax.rem(self.c + COLS - 1, COLS)},
            "yf": {"col": lax.rem(self.c + 2, COLS)},
            "xr": {"depth": lax.rem(self.d + 1, DEPTHS)},
            "xl": {"depth": lax.rem(self.d + DEPTHS - 1, DEPTHS)},
            "xf": {"depth": lax.rem(self.d + 2, DEPTHS)},
        }
        other = 1 - 2 * self.core
        self.peers["zrs"] = {"row": lax.rem(self.r + 2 + other, ROWS)}
        self.peers["zls"] = {"row": lax.rem(self.r + ROWS - 2 + other, ROWS)}
        for k in (2, 3, 4, 5, 6):
            self.peers["z%d" % k] = {"row": lax.rem(self.r + 2 * k, ROWS)}
        self.peers["z1"], self.peers["z7"] = self.peers["zr"], self.peers["zl"]

    def barrier(self, names):
        bar = pltpu.get_barrier_semaphore()
        for name in names:
            pl.semaphore_signal(
                bar, inc=1, device_id=self.peers[name], device_id_type=pl.DeviceIdType.MESH
            )
        pl.semaphore_wait(bar, len(names))

    def send(self, src, dst, name):
        i = self.count
        self.count += 1
        copy = pltpu.make_async_remote_copy(
            src_ref=src,
            dst_ref=dst,
            send_sem=self.ssem.at[i],
            recv_sem=self.rsem.at[i],
            device_id=self.peers[name],
            device_id_type=pl.DeviceIdType.MESH,
        )
        copy.start()
        self.sent.append(copy)
        return copy

    def release(self, copies):
        for copy in copies:
            copy.wait_send()
        self.sent = [one for one in self.sent if all(one is not copy for copy in copies)]

    def finish(self):
        for copy in self.sent:
            copy.wait_send()

    def zk(self, k):
        return lax.rem(self.z + k % RING, RING)


def ring_gather(net, slot, part_a, part_b, arrived, both=None):
    pend = {}
    pend["ra", 0] = net.send(slot(net.z, part_a), slot(net.z, part_a), "zr")
    pend["lb", 0] = net.send(slot(net.z, part_b), slot(net.z, part_b), "zl")
    pend["rb", 0] = net.send(slot(net.z, part_b), slot(net.z, part_b), "zr")
    pend["la", 0] = net.send(slot(net.z, part_a), slot(net.z, part_a), "zl")

    def step(s):
        for key, far in (("ra", 4), ("lb", 4), ("rb", 3), ("la", 3)):
            if s >= far:
                continue
            pend[key, s].wait_recv()
            k = -(s + 1) if key[0] == "r" else s + 1
            part = part_a if key[1] == "a" else part_b
            ref = slot(net.zk(k), part)
            if s + 1 < far:
                pend[key, s + 1] = net.send(ref, ref, "zr" if key[0] == "r" else "zl")
            if both is not None and s == 2 and far == 4:
                both[key] = net.send(ref, ref, "zrs" if key[0] == "r" else "zls")
            arrived(s, k, key[1], ref)

    return step


class WeightSum:
    def __init__(self, net, width, xt, xg, rows, acc, dw, dwsib):
        self.net, self.width, self.xt, self.xg, self.rows = net, width, xt, xg, rows
        self.acc, self.dw, self.dwsib = acc, dw, dwsib
        self.swap = {}

    def multiply(self, sources, first, last):
        def group(g, carry):
            at = pl.ds(2 * g, 2)
            total = None if first else self.acc[at].reshape(256, self.width)
            for i in sources:
                x = self.xg[i - 1, at] if i else self.xt[at, :, self.net.d]
                part = jnp.dot(x.reshape(256, TOK), self.rows[i], preferred_element_type=F32)
                total = part if total is None else total + part
            if last:
                self.dw[at] = total.astype(BF16).reshape(2, 2, 64, self.width)
            else:
                self.acc[at] = total.reshape(2, 2, 64, self.width)
            return carry

        lax.fori_loop(0, RING // 2, group, 0)

    def trade(self):
        net = self.net
        for k in (4, 3, -3, 2, -2, 1, -1, 0):
            zz = net.zk(k)
            self.swap[k] = net.send(self.dw.at[zz, 1 - net.core], self.dwsib.at[zz], "sib")

    def fold(self, k):
        zz = self.net.zk(k)
        self.swap[k].wait_recv()
        add(self.dw.at[zz, self.net.core], self.dwsib.at[zz])


class RingSum(WeightSum):
    def __init__(self, zin, *rest):
        super().__init__(*rest)
        self.zin, self.got = zin, {}

    def half(self, k, half):
        return self.dw.at[self.net.zk(k), self.net.core, pl.ds(32 * half, 32)]

    def out(self, way, half, n):
        self.got[way, half, n] = self.net.send(
            self.half(n if way == "r" else -n, half),
            self.zin.at[0 if way == "r" else 1, half, n - 1],
            "zr" if way == "r" else "zl",
        )

    def take(self, way, half, n):
        self.got[way, half, n].wait_recv()
        add(
            self.half(n - 1 if way == "r" else 1 - n, half),
            self.zin.at[0 if way == "r" else 1, half, n - 1],
        )

    def start(self):
        self.fold(4)
        self.out("r", 0, 4)
        self.out("l", 1, 4)
        self.fold(3)
        self.out("r", 1, 3)
        self.fold(-3)
        self.out("l", 0, 3)

    def second(self):
        self.take("r", 0, 4)
        self.out("r", 0, 3)
        self.take("l", 1, 4)
        self.out("l", 1, 3)

    def later(self, n):
        self.fold(n)
        self.fold(-n)
        for way, half in (("r", 1), ("l", 0), ("r", 0), ("l", 1)):
            self.take(way, half, n + 1)
            self.out(way, half, n)

    def result(self):
        self.fold(0)
        net, parts = self.net, []
        for half in range(2):
            total = self.half(0, half)[...].astype(F32)
            for way in range(2):
                self.got["rl"[way], half, 1].wait_recv()
                total = total + self.zin[way, half, 0].astype(F32)
            parts.append(total)
        return parts


class DirectSum(WeightSum):
    def __init__(self, zin, *rest):
        super().__init__(*rest)
        self.zin, self.got = zin, []

    def start(self):
        net = self.net
        for k in (4, 3, -3, 2, -2, 1, -1):
            self.fold(k)
            self.got.append(
                net.send(
                    self.dw.at[net.zk(k), net.core],
                    self.zin.at[k % RING - 1],
                    "z%d" % (k % RING),
                )
            )
        self.fold(0)

    def result(self):
        total = self.dw[self.net.z, self.net.core].astype(F32)
        for copy in self.got:
            copy.wait_recv()
        for i in range(RING - 1):
            total = total + self.zin[i].astype(F32)
        return total


def add(ref, src):
    ref[...] = (ref[...].astype(F32) + src[...].astype(F32)).astype(BF16)


def fused_kernel(
    x_hbm, wq_hbm, wk_hbm, wv_hbm, go_hbm, gi_ref, gq_ref, gk_ref, gv_ref,
    xf, wqf, wkf, xt, kvb, qh, oh, prob, gprob, mblk, stat, dqt, part, fromsib, rin, rlate,
    rq, rkx, rky, xg, wkv, yin, accq, dwq, dwqsib, zqin, acck, dwk, dwksib, zkin,
    ssem, rsem, lsem,
):
    net = Net(ssem, rsem)
    c, d, z, core = net.c, net.d, net.z, net.core
    left, right, far = lax.rem(c + 3, COLS), lax.rem(c + 1, COLS), lax.rem(c + 2, COLS)
    own_q, own_k = wqf.at[z, core], wkf.at[z, core]
    local = []

    def fetch(src, dst):
        copy = pltpu.make_async_copy(src, dst, lsem.at[len(local)])
        copy.start()
        local.append(copy)

    fetch(wk_hbm, own_k.at[:, :, pl.ds(0, 128)])
    fetch(wv_hbm, own_k.at[:, :, pl.ds(128, 128)])
    fetch(wq_hbm, own_q)
    fetch(x_hbm, xf.at[c])
    for s in range(2):
        for h in range(GROUP):
            fetch(go_hbm.at[s, :, pl.ds(h * 128, 128)], oh.at[s, pl.ds(h * 128, 128)])
    net.barrier(
        ["zr", "zl", "sib", "yr", "yl", "yf", "xr", "xl", "xf"]
        + ["z2", "z3", "z4", "z5", "z6", "zrs", "zls"]
    )
    for copy in local[:4]:
        copy.wait()

    class Spread:
        def __init__(self, full):
            self.full, self.sib, self.cross = full, [], {}
            own = full.at[z, core]
            self.step = ring_gather(
                net,
                lambda zz, q: full.at[zz, core, q],
                d,
                lax.rem(d + 1, DEPTHS),
                self.arrived,
            )
            self.sib.append(net.send(own, own, "sib"))

        def arrived(self, s, k, half, ref):
            self.cross[k, half] = net.send(ref, ref, "xr" if half == "a" else "xl")
            self.sib.append(net.send(ref, ref, "sib"))

        def crossed(self, s):
            for k in (-(s + 1), s + 1):
                for half in ("a", "b"):
                    if s == 3 and (k > 0) != (half == "b"):
                        continue
                    self.cross[k, half].wait_recv()
                    q = lax.rem(d + (3 if half == "a" else 2), DEPTHS)
                    ref = self.full.at[net.zk(k), core, q]
                    self.sib.append(net.send(ref, ref, "sib"))

        def complete(self):
            for copy in self.sib:
                copy.wait_recv()

    wk = Spread(wkf)
    ya_r = net.send(xf.at[c, 0], xf.at[c, 0], "yr")
    yb_l = net.send(xf.at[c, 1], xf.at[c, 1], "yl")
    yb_r = net.send(xf.at[c, 1], xf.at[c, 1], "yr")
    ya_l = net.send(xf.at[c, 0], xf.at[c, 0], "yl")
    wq = Spread(wqf)

    def transpose(cc):
        for s in range(2):
            for k in range(DCOL // 128):
                xt[
                    2 * cc + k // 4,
                    (k % 4) // 2,
                    2 * (k % 2) : 2 * (k % 2) + 2,
                    :,
                    s * 128 : (s + 1) * 128,
                ] = xf[cc, s, :, k * 128 : (k + 1) * 128].T.reshape(2, 64, 128)

    xg_got = [[], [], []]

    def hand_round(cc):
        for i, (n, name) in enumerate(((2, "xf"), (1, "xr"), (3, "xl"))):
            at = pl.ds(2 * cc, 2)
            quarter = lax.rem(d + n, DEPTHS)
            xg_got[i].append(net.send(xt.at[at, :, quarter], xg.at[i, at], name))

    transpose(c)
    wk.step(0)
    wq.step(0)
    wk.step(1)
    wk.crossed(0)
    ya_r.wait_recv()
    y2a = net.send(xf.at[left, 0], xf.at[left, 0], "yr")
    yb_l.wait_recv()
    y2b = net.send(xf.at[right, 1], xf.at[right, 1], "yl")
    wq.step(1)
    wq.crossed(0)
    wk.step(2)
    wk.crossed(1)
    wq.step(2)
    wq.crossed(1)
    wk.step(3)
    wk.crossed(2)
    yb_r.wait_recv()
    ya_l.wait_recv()
    transpose(left)
    transpose(right)
    wq.step(3)
    wk.crossed(3)
    wq.crossed(2)
    wk.complete()

    def project(chunks, full, width):
        total = None
        for cc in chunks:
            w = full[pl.ds(2 * cc, 2)].reshape(DCOL, width)
            part = jnp.dot(xf[cc].reshape(TOK, DCOL), w, preferred_element_type=F32)
            total = part if total is None else total + part
        return total

    near = project((c, left, right), wkf, KVW)
    y2a.wait_recv()
    y2b.wait_recv()
    near = (near + project((far,), wkf, KVW)).astype(BF16)

    def slot(zz, half):
        return kvb.at[zz, half, core]

    kvb[z, 0, core] = near[:SEQ_TOK]
    kvb[z, 1, core] = near[SEQ_TOK:]
    kvsib = {}

    def kv_arrived(s, k, half, ref):
        if s < 3:
            kvsib[k % RING, half] = net.send(ref, ref, "sib")

    kvsib[0, "a"] = net.send(slot(z, 0), slot(z, 0), "sib")
    kvsib[0, "b"] = net.send(slot(z, 1), slot(z, 1), "sib")
    kvboth = {}
    step = ring_gather(net, slot, 0, 1, kv_arrived, kvboth)

    wkv_got = []
    for i, (cc, name) in enumerate(((far, "yf"), (right, "yr"), (left, "yl"))):
        wkv_got.append(net.send(wkf.at[pl.ds(2 * cc, 2), core], wkv.at[i, core], name))
    transpose(far)
    for cc in (c, left, right, far):
        hand_round(cc)
    wq.crossed(3)
    step(0)
    wq.complete()
    query = project((c, left, right, far), wqf, QW).astype(BF16)
    for s in range(2):
        for h in range(GROUP):
            qh[s, h * 128 : (h + 1) * 128] = query[
                s * 128 : (s + 1) * 128, h * 128 : (h + 1) * 128
            ]
    for copy in local[4:]:
        copy.wait()
    net.release((ya_r, yb_l, yb_r, ya_l, y2a, y2b))

    def scores(s, zz):
        kv = kvb[zz, s].reshape(2 * SEQ_TOK, KVW)
        st = lax.dot_general(kv[:, :HEAD_DIM], qh[s], NT, preferred_element_type=F32)
        dp = lax.dot_general(kv[:, HEAD_DIM:], oh[s], NT, preferred_element_type=F32)
        return st * EXP_SCALE, dp

    def begin(s, carry):
        st, dp = scores(s, z)
        key = lax.broadcasted_iota(jnp.int32, (2 * SEQ_TOK, QW), 0)
        query_pos = lax.rem(lax.broadcasted_iota(jnp.int32, (2 * SEQ_TOK, QW), 1), SEQ_TOK)
        st = jnp.where(key <= query_pos + core * SEQ_TOK, st, -1e30)
        m = jnp.max(st, 0, keepdims=True)
        p = jnp.exp2(st - m)
        prob[z, s] = p
        gprob[z, s] = dp
        mblk[z, s] = m
        stat[s, 0:1] = m
        stat[s, 1:2] = jnp.sum(p, 0, keepdims=True)
        stat[s, 2:3] = jnp.sum(p * dp, 0, keepdims=True)
        return carry

    def more(zz):
        def one(s, carry):
            st, dp = scores(s, zz)
            old = stat[s, 0:1]
            m = jnp.maximum(old, jnp.max(st, 0, keepdims=True))
            p = jnp.exp2(st - m)
            fade = jnp.exp2(old - m)
            prob[zz, s] = p
            gprob[zz, s] = dp
            mblk[zz, s] = m
            stat[s, 0:1] = m
            stat[s, 1:2] = stat[s, 1:2] * fade + jnp.sum(p, 0, keepdims=True)
            stat[s, 2:3] = stat[s, 2:3] * fade + jnp.sum(p * dp, 0, keepdims=True)
            return carry

        @pl.when(zz < z)
        def _():
            lax.fori_loop(0, 2, one, 0)

    kvsib[0, "a"].wait_recv()
    kvsib[0, "b"].wait_recv()
    lax.fori_loop(0, 2, begin, 0)
    part[...] = jnp.zeros_like(part)
    dqt[...] = jnp.zeros_like(dqt)
    for s in range(4):
        if s:
            step(s)
        for k in (-(s + 1), s + 1) if s < 3 else (4,):
            for half in ("a", "b"):
                if s < 3:
                    kvsib[k % RING, half].wait_recv()
                else:
                    kvboth["ra" if half == "a" else "lb"].wait_recv()
            more(net.zk(k))

    for s in range(2):
        inv = 1.0 / stat[s, 1:2]
        stat[s, 3:4] = inv
        stat[s, 4:5] = stat[s, 2:3] * inv

    def back_block(zz):
        for s in range(2):
            fac = jnp.exp2(mblk[zz, s] - stat[s, 0:1]) * stat[s, 3:4]
            p = prob[zz, s] * fac
            low = p.astype(BF16)
            ds = (p * (gprob[zz, s] - stat[s, 4:5])).astype(BF16)
            dv = jnp.dot(low, oh[s], preferred_element_type=F32)
            dk = jnp.dot(ds, qh[s], preferred_element_type=F32) * SCALE
            keys = kvb[zz, s].reshape(2 * SEQ_TOK, KVW)[:, :HEAD_DIM]
            dqt[s] += jnp.dot(keys.T, ds, preferred_element_type=F32)
            for co in range(2):
                part[zz, co, s, :, :HEAD_DIM] = dk[co * 128 : (co + 1) * 128].astype(BF16)
                part[zz, co, s, :, HEAD_DIM:] = dv[co * 128 : (co + 1) * 128].astype(BF16)

    swap = {}

    def back(n):
        def one(i, carry):
            zz = lax.rem(z + n + i * (2 * RING - 2 * n), RING)

            @pl.when(zz <= z)
            def _():
                back_block(zz)

            return carry

        ks = (n, -n) if n % 4 else (n,)
        lax.fori_loop(0, len(ks), one, 0)
        for k in ks if n % 4 or not n else ():
            swap[k] = net.send(part.at[net.zk(k), 1 - core], fromsib.at[net.zk(k)], "sib")

    def fold(k):
        swap[k].wait_recv()
        add(part.at[net.zk(k), core], fromsib.at[net.zk(k)])

    got = {}

    def out(way, half, n):
        got[way, half, n] = net.send(
            part.at[net.zk(n if way == "r" else -n), core, half],
            rin.at[0 if way == "r" else 1, half, n - 1],
            "zr" if way == "r" else "zl",
        )

    def take(way, half, n):
        got[way, half, n].wait_recv()
        add(
            part.at[net.zk(n - 1 if way == "r" else 1 - n), core, half],
            rin.at[0 if way == "r" else 1, half, n - 1],
        )

    def later(n):
        fold(n)
        fold(-n)
        for way, half in (("r", 1), ("l", 0), ("r", 0), ("l", 1)):
            take(way, half, n + 1)
            out(way, half, n)

    back(4)
    out("r", 0, 4)
    out("l", 1, 4)
    late = []
    for half, name in enumerate(("zrs", "zls")):
        late.append(net.send(part.at[net.zk(4), 1 - core, half], rlate.at[half], name))
    back(3)
    back(2)
    fold(3)
    fold(-3)
    out("r", 1, 3)
    out("l", 0, 3)
    back(1)
    back(0)

    for s in range(2):
        for h in range(GROUP):
            rq[0, s * 128 : (s + 1) * 128, h * 128 : (h + 1) * 128] = (
                (dqt[s, :, h * 128 : (h + 1) * 128] * SCALE).T.astype(BF16)
            )

    top, low = pl.ds(0, SEQ_TOK), pl.ds(SEQ_TOK, SEQ_TOK)
    rqa_r = net.send(rq.at[0, top], rq.at[2, top], "xr")
    rqb_l = net.send(rq.at[0, low], rq.at[3, low], "xl")
    rqb_r = net.send(rq.at[0, low], rq.at[2, low], "xr")
    rqa_l = net.send(rq.at[0, top], rq.at[3, top], "xl")

    def input_part(cc):
        w = wqf[pl.ds(2 * cc, 2)].reshape(DCOL, QW)
        return lax.dot_general(rq[0], w, NT, preferred_element_type=F32)

    def input_store(i, cc):
        xf[i] = input_part(cc).astype(BF16).reshape(2, SEQ_TOK, DCOL)

    to_far, to_right, to_left = xf.at[0], xf.at[1], xf.at[2]
    input_store(0, far)
    y0 = net.send(to_far.at[0], yin.at[0], "yr")
    y1 = net.send(to_far.at[1], yin.at[1], "yl")
    for way, half, k in (("r", 0, 3), ("l", 1, -3)):
        take(way, half, 4)
        late[half].wait_recv()
        add(part.at[net.zk(k), core, half], rlate.at[half])
        out(way, half, 3)
    input_store(1, right)
    y2 = net.send(to_right.at[1], yin.at[2], "yr")
    input_store(2, left)
    y3 = net.send(to_left.at[0], yin.at[3], "yl")

    wsq = RingSum(zqin, net, QW, xt, xg, rq, accq, dwq, dwqsib)
    wsk = DirectSum(zkin, net, KVW, xt, xg, rkx, acck, dwk, dwksib)
    wkv_sib = []
    for i, copy in enumerate(wkv_got):
        copy.wait_recv()
        wkv_sib.append(net.send(wkv.at[i, core], wkv.at[i, core], "sib"))
    wsq.multiply((0,), True, False)
    later(2)
    rqa_r.wait_recv()
    rqa_f = net.send(rq.at[2, top], rq.at[1, top], "xr")
    rqb_l.wait_recv()
    rqb_f = net.send(rq.at[3, low], rq.at[1, low], "xl")
    later(1)
    y0.wait_recv()
    add(to_right.at[0], yin.at[0])
    y4 = net.send(to_right.at[0], yin.at[4], "yr")
    y1.wait_recv()
    add(to_left.at[1], yin.at[1])
    y5 = net.send(to_left.at[1], yin.at[5], "yl")
    total_own = input_part(c)
    fold(0)
    for half in range(2):
        total = part[z, core, half].astype(F32)
        for way in range(2):
            got["rl"[way], half, 1].wait_recv()
            total = total + rin[way, half, 0].astype(F32)
        rkx[0, half * 128 : (half + 1) * 128] = total.astype(BF16)
    rkx_got = [net.send(rkx.at[0], rkx.at[i + 1], ("xf", "xr", "xl")[i]) for i in range(3)]
    rky_got = [net.send(rkx.at[0], rky.at[i], ("yf", "yr", "yl")[i]) for i in range(3)]
    wsk.multiply((0,), True, False)
    for i in (1, 2):
        for copy in xg_got[i]:
            copy.wait_recv()
    rqb_r.wait_recv()
    rqa_l.wait_recv()
    wsq.multiply((2, 3), False, False)
    for copy in xg_got[0]:
        copy.wait_recv()
    rqa_f.wait_recv()
    rqb_f.wait_recv()
    wsq.multiply((1,), False, True)
    wsq.trade()
    wsq.start()
    for copy in wkv_sib:
        copy.wait_recv()
    total = total_own
    for i in (1, 2):
        rkx_got[i].wait_recv()
    wsk.multiply((2, 3), False, False)
    wsq.second()
    rkx_got[0].wait_recv()
    wsk.multiply((1,), False, True)
    wsk.trade()
    wsq.later(2)
    wsk.start()
    wsq.later(1)

    def key_share(rows, w):
        return lax.dot_general(rows, w.reshape(DCOL, KVW), NT, preferred_element_type=F32)

    total = total + key_share(rkx[0], wkf[pl.ds(2 * c, 2)])
    for i in range(3):
        rky_got[i].wait_recv()
        total = total + key_share(rky[i], jnp.stack([wkv[i, 0], wkv[i, 1]], 1))
    for copy in (y2, y3, y4, y5):
        copy.wait_recv()
    gi_ref[0] = (total[:SEQ_TOK] + yin[3].astype(F32) + yin[4].astype(F32)).astype(BF16)
    gi_ref[1] = (total[SEQ_TOK:] + yin[2].astype(F32) + yin[5].astype(F32)).astype(BF16)
    gkv = wsk.result()
    gk_ref[...] = gkv[:, :HEAD_DIM]
    gv_ref[...] = gkv[:, HEAD_DIM:]
    first, second = wsq.result()
    gq_ref[:32] = first
    gq_ref[32:] = second
    net.finish()
    assert net.count <= COPIES, net.count


def deliver_kernel(*refs):
    for src, dst in zip(refs[:4], refs[4:]):
        dst[...] = src[...]


def body(inputs, w_query, w_key, w_value, grad_out):
    vm = pl.BlockSpec(memory_space=pltpu.VMEM)
    hbm = pl.BlockSpec(memory_space=pltpu.HBM)
    results = pl.pallas_call(
        fused_kernel,
        name="fused",
        out_shape=(
            jax.ShapeDtypeStruct((2, SEQ_TOK, DCOL), BF16),
            jax.ShapeDtypeStruct((64, QW), F32),
            jax.ShapeDtypeStruct((64, HEAD_DIM), F32),
            jax.ShapeDtypeStruct((64, HEAD_DIM), F32),
        ),
        in_specs=[hbm] * 5,
        out_specs=(vm,) * 4,
        scratch_shapes=[
            pltpu.VMEM((COLS, 2, SEQ_TOK, DCOL), BF16),
            pltpu.VMEM((RING, 2, 4, 64, QW), BF16),
            pltpu.VMEM((RING, 2, 4, 64, KVW), BF16),
            pltpu.VMEM((RING, 2, 4, 64, TOK), BF16),
            pltpu.VMEM((RING, 2, 2, SEQ_TOK, KVW), BF16),
            pltpu.VMEM((2, QW, HEAD_DIM), BF16),
            pltpu.VMEM((2, QW, HEAD_DIM), BF16),
            pltpu.VMEM((RING, 2, 2 * SEQ_TOK, QW), F32),
            pltpu.VMEM((RING, 2, 2 * SEQ_TOK, QW), F32),
            pltpu.VMEM((RING, 2, 1, QW), F32),
            pltpu.VMEM((2, 8, QW), F32),
            pltpu.VMEM((2, HEAD_DIM, QW), F32),
            pltpu.VMEM((RING, 2, 2, SEQ_TOK, KVW), BF16),
            pltpu.VMEM((RING, 2, SEQ_TOK, KVW), BF16),
            pltpu.VMEM((2, 2, 4, SEQ_TOK, KVW), BF16),
            pltpu.VMEM((2, SEQ_TOK, KVW), BF16),
            pltpu.VMEM((DEPTHS, TOK, QW), BF16),
            pltpu.VMEM((DEPTHS, TOK, KVW), BF16),
            pltpu.VMEM((3, TOK, KVW), BF16),
            pltpu.VMEM((3, RING, 2, 64, TOK), BF16),
            pltpu.VMEM((3, 2, 2, 4, 64, KVW), BF16),
            pltpu.VMEM((6, SEQ_TOK, DCOL), BF16),
            pltpu.VMEM((RING, 2, 64, QW), F32),
            pltpu.VMEM((RING, 2, 64, QW), BF16),
            pltpu.VMEM((RING, 64, QW), BF16),
            pltpu.VMEM((2, 2, 4, 32, QW), BF16),
            pltpu.VMEM((RING, 2, 64, KVW), F32),
            pltpu.VMEM((RING, 2, 64, KVW), BF16),
            pltpu.VMEM((RING, 64, KVW), BF16),
            pltpu.VMEM((RING - 1, 64, KVW), BF16),
            pltpu.SemaphoreType.DMA((COPIES,)),
            pltpu.SemaphoreType.DMA((COPIES,)),
            pltpu.SemaphoreType.DMA((16,)),
        ],
        compiler_params=pltpu.CompilerParams(
            collective_id=0, has_side_effects=True, vmem_limit_bytes=57 << 20
        ),
    )(
        inputs,
        w_query.reshape(4, 64, QW),
        w_key.reshape(4, 64, HEAD_DIM),
        w_value.reshape(4, 64, HEAD_DIM),
        grad_out,
    )
    return pl.pallas_call(
        deliver_kernel,
        name="deliver",
        out_shape=[jax.ShapeDtypeStruct(one.shape, one.dtype) for one in results],
        in_specs=[vm] * 4,
        out_specs=[vm] * 4,
    )(*results)


def solution(mesh):
    return jax.shard_map(
        body,
        mesh=mesh,
        in_specs=(
            P("depth", "row", "col"),
            P("row", "col"),
            P("row", "col"),
            P("row", "col"),
            P("depth", "row", "col"),
        ),
        out_specs=(
            P("depth", "row", "col"),
            P(("row", "depth"), "col"),
            P(("row", "depth"), "col"),
            P(("row", "depth"), "col"),
        ),
        check_vma=False,
    )
```

```python
import functools

import jax
import jax.numpy as jnp
from jax import lax
from jax.experimental import pallas as pl
from jax.experimental.pallas import tpu as pltpu
from jax.sharding import PartitionSpec as P

HEAD_DIM = 128
ROWS, COLS, DEPTHS = 16, 4, 4
RING = ROWS // 2
TOK = 256
SEQ_TOK = 128
GROUP = 4
QW = 512
WIDTH = 768
KVW = 256
COPIES = 288
DCOL = 1024
TILE = 256
BF16, F32 = jnp.bfloat16, jnp.float32
SCALE = HEAD_DIM ** -0.5
EXP_SCALE = SCALE * 1.4426950408889634
NT = (((1,), (1,)), ((), ()))


class Net:
    def __init__(self, ssem, rsem):
        self.r = lax.axis_index("row")
        self.c = lax.axis_index("col")
        self.d = lax.axis_index("depth")
        self.z = self.r // 2
        self.core = lax.rem(self.r, 2)
        self.ssem, self.rsem = ssem, rsem
        self.count = 0
        self.sent = []
        self.peers = {
            "zr": {"row": lax.rem(self.r + 2, ROWS)},
            "zl": {"row": lax.rem(self.r + ROWS - 2, ROWS)},
            "sib": {"row": self.r + 1 - 2 * self.core},
            "yr": {"col": lax.rem(self.c + 1, COLS)},
            "yl": {"col": lax.rem(self.c + COLS - 1, COLS)},
            "yf": {"col": lax.rem(self.c + 2, COLS)},
            "xr": {"depth": lax.rem(self.d + 1, DEPTHS)},
            "xl": {"depth": lax.rem(self.d + DEPTHS - 1, DEPTHS)},
            "xf": {"depth": lax.rem(self.d + 2, DEPTHS)},
        }
        other = 1 - 2 * self.core
        self.peers["zrs"] = {"row": lax.rem(self.r + 2 + other, ROWS)}
        self.peers["zls"] = {"row": lax.rem(self.r + ROWS - 2 + other, ROWS)}
        for k in (2, 3, 4, 5, 6):
            self.peers["z%d" % k] = {"row": lax.rem(self.r + 2 * k, ROWS)}
        self.peers["z1"], self.peers["z7"] = self.peers["zr"], self.peers["zl"]

    def greet(self, names):
        bar = pltpu.get_barrier_semaphore()
        for name in names:
            pl.semaphore_signal(
                bar, inc=1, device_id=self.peers[name], device_id_type=pl.DeviceIdType.MESH
            )
        return len(names)

    def send(self, src, dst, name):
        i = self.count
        self.count += 1
        copy = pltpu.make_async_remote_copy(
            src_ref=src,
            dst_ref=dst,
            send_sem=self.ssem.at[i],
            recv_sem=self.rsem.at[i],
            device_id=self.peers[name],
            device_id_type=pl.DeviceIdType.MESH,
        )
        copy.start()
        self.sent.append(copy)
        return copy

    def release(self, copies):
        for copy in copies:
            copy.wait_send()
        self.sent = [one for one in self.sent if all(one is not copy for copy in copies)]

    def finish(self):
        for copy in self.sent:
            copy.wait_send()

    def zk(self, k):
        return lax.rem(self.z + k % RING, RING)


def ring_gather(net, slot, part_a, part_b, arrived, both=None):
    pend = {}
    pend["ra", 0] = net.send(slot(net.z, part_a), slot(net.z, part_a), "zr")
    pend["lb", 0] = net.send(slot(net.z, part_b), slot(net.z, part_b), "zl")
    pend["rb", 0] = net.send(slot(net.z, part_b), slot(net.z, part_b), "zr")
    pend["la", 0] = net.send(slot(net.z, part_a), slot(net.z, part_a), "zl")

    def step(s):
        for key, far in (("ra", 4), ("lb", 4), ("rb", 3), ("la", 3)):
            if s >= far:
                continue
            pend[key, s].wait_recv()
            k = -(s + 1) if key[0] == "r" else s + 1
            part = part_a if key[1] == "a" else part_b
            ref = slot(net.zk(k), part)
            if s + 1 < far:
                pend[key, s + 1] = net.send(ref, ref, "zr" if key[0] == "r" else "zl")
            if both is not None and s == 2 and far == 4:
                both[key] = net.send(ref, ref, "zrs" if key[0] == "r" else "zls")
            arrived(s, k, key[1], ref)

    return step


class WeightSum:
    def __init__(self, net, width, xt, xg, rows, acc, dw, dwsib):
        self.net, self.width, self.xt, self.xg, self.rows = net, width, xt, xg, rows
        self.acc, self.dw, self.dwsib = acc, dw, dwsib
        self.swap = {}

    def multiply(self, sources, first, last):
        def group(g, carry):
            at = pl.ds(2 * g, 2)
            total = None if first else self.acc[at].reshape(256, self.width)
            for i in sources:
                x = self.xg[i - 1, at] if i else self.xt[at, :, self.net.d]
                part = jnp.dot(x.reshape(256, TOK), self.rows[i], preferred_element_type=F32)
                total = part if total is None else total + part
            if last:
                self.dw[at] = total.astype(BF16).reshape(2, 2, 64, self.width)
            else:
                self.acc[at] = total.reshape(2, 2, 64, self.width)
            return carry

        lax.fori_loop(0, RING // 2, group, 0)

    def trade(self):
        net = self.net
        for k in (4, 3, -3, 2, -2, 1, -1, 0):
            zz = net.zk(k)
            self.swap[k] = net.send(self.dw.at[zz, 1 - net.core], self.dwsib.at[zz], "sib")

    def fold(self, k):
        zz = self.net.zk(k)
        self.swap[k].wait_recv()
        add(self.dw.at[zz, self.net.core], self.dwsib.at[zz])


class RingSum(WeightSum):
    def __init__(self, zin, *rest):
        super().__init__(*rest)
        self.zin, self.got = zin, {}

    def half(self, k, half):
        return self.dw.at[self.net.zk(k), self.net.core, pl.ds(32 * half, 32)]

    def out(self, way, half, n):
        self.got[way, half, n] = self.net.send(
            self.half(n if way == "r" else -n, half),
            self.zin.at[0 if way == "r" else 1, half, n - 1],
            "zr" if way == "r" else "zl",
        )

    def take(self, way, half, n):
        self.got[way, half, n].wait_recv()
        add(
            self.half(n - 1 if way == "r" else 1 - n, half),
            self.zin.at[0 if way == "r" else 1, half, n - 1],
        )

    def start(self):
        self.fold(4)
        self.out("r", 0, 4)
        self.out("l", 1, 4)
        self.fold(3)
        self.out("r", 1, 3)
        self.fold(-3)
        self.out("l", 0, 3)

    def second(self):
        self.take("r", 0, 4)
        self.out("r", 0, 3)
        self.take("l", 1, 4)
        self.out("l", 1, 3)

    def later(self, n):
        self.fold(n)
        self.fold(-n)
        for way, half in (("r", 1), ("l", 0), ("r", 0), ("l", 1)):
            self.take(way, half, n + 1)
            self.out(way, half, n)

    def result(self):
        self.fold(0)
        net, parts = self.net, []
        for half in range(2):
            total = self.half(0, half)[...].astype(F32)
            for way in range(2):
                self.got["rl"[way], half, 1].wait_recv()
                total = total + self.zin[way, half, 0].astype(F32)
            parts.append(total)
        return parts


class DirectSum(WeightSum):
    def __init__(self, zin, *rest):
        super().__init__(*rest)
        self.zin, self.got = zin, []

    def start(self):
        net = self.net
        for k in (4, 3, -3, 2, -2, 1, -1):
            self.fold(k)
            self.got.append(
                net.send(
                    self.dw.at[net.zk(k), net.core],
                    self.zin.at[k % RING - 1],
                    "z%d" % (k % RING),
                )
            )
        self.fold(0)

    def result(self):
        total = self.dw[self.net.z, self.net.core].astype(F32)
        for copy in self.got:
            copy.wait_recv()
        for i in range(RING - 1):
            total = total + self.zin[i].astype(F32)
        return total


def add(ref, src):
    ref[...] = (ref[...].astype(F32) + src[...].astype(F32)).astype(BF16)


def fused_kernel(
    x_hbm, wq_hbm, wk_hbm, wv_hbm, go_hbm, gi_ref, gq_ref, gk_ref, gv_ref,
    xf, wqf, wkf, xt, kvb, qh, oh, prob, gprob, mblk, stat, dqt, part, fromsib, rin, rlate,
    rq, rkx, rky, xg, wkv, yin, accq, dwq, dwqsib, zqin, acck, dwk, dwksib, zkin,
    ssem, rsem, lsem,
):
    net = Net(ssem, rsem)
    c, d, z, core = net.c, net.d, net.z, net.core
    left, right, far = lax.rem(c + 3, COLS), lax.rem(c + 1, COLS), lax.rem(c + 2, COLS)
    expected = net.greet(
        ["zr", "zl", "sib", "yr", "yl", "yf", "xr", "xl", "xf"]
        + ["z2", "z3", "z4", "z5", "z6", "zrs", "zls"]
    )
    own_q, own_k = wqf.at[z, core], wkf.at[z, core]
    local = []

    def fetch(src, dst):
        copy = pltpu.make_async_copy(src, dst, lsem.at[len(local)])
        copy.start()
        local.append(copy)

    fetch(x_hbm, xf.at[c])
    fetch(wk_hbm, own_k.at[:, :, pl.ds(0, 128)])
    fetch(wv_hbm, own_k.at[:, :, pl.ds(128, 128)])
    fetch(wq_hbm, own_q)
    pl.semaphore_wait(pltpu.get_barrier_semaphore(), expected)
    for copy in local[:4]:
        copy.wait()

    class Spread:
        def __init__(self, full):
            self.full, self.sib, self.cross = full, [], {}
            own = full.at[z, core]
            self.step = ring_gather(
                net,
                lambda zz, q: full.at[zz, core, q],
                d,
                lax.rem(d + 1, DEPTHS),
                self.arrived,
            )
            self.sib.append(net.send(own, own, "sib"))

        def arrived(self, s, k, half, ref):
            self.cross[k, half] = net.send(ref, ref, "xr" if half == "a" else "xl")
            self.sib.append(net.send(ref, ref, "sib"))

        def crossed(self, s):
            for k in (-(s + 1), s + 1):
                for half in ("a", "b"):
                    if s == 3 and (k > 0) != (half == "b"):
                        continue
                    self.cross[k, half].wait_recv()
                    q = lax.rem(d + (3 if half == "a" else 2), DEPTHS)
                    ref = self.full.at[net.zk(k), core, q]
                    self.sib.append(net.send(ref, ref, "sib"))

        def complete(self):
            for copy in self.sib:
                copy.wait_recv()

    wk = Spread(wkf)
    ya_r = net.send(xf.at[c, 0], xf.at[c, 0], "yr")
    yb_l = net.send(xf.at[c, 1], xf.at[c, 1], "yl")
    yb_r = net.send(xf.at[c, 1], xf.at[c, 1], "yr")
    ya_l = net.send(xf.at[c, 0], xf.at[c, 0], "yl")
    wq = Spread(wqf)

    def transpose(cc):
        for s in range(2):
            for k in range(DCOL // 128):
                xt[
                    2 * cc + k // 4,
                    (k % 4) // 2,
                    2 * (k % 2) : 2 * (k % 2) + 2,
                    :,
                    s * 128 : (s + 1) * 128,
                ] = xf[cc, s, :, k * 128 : (k + 1) * 128].T.reshape(2, 64, 128)

    xg_got = [[], [], []]

    def hand_round(cc):
        for i, (n, name) in enumerate(((2, "xf"), (1, "xr"), (3, "xl"))):
            at = pl.ds(2 * cc, 2)
            quarter = lax.rem(d + n, DEPTHS)
            xg_got[i].append(net.send(xt.at[at, :, quarter], xg.at[i, at], name))

    for s in range(2):
        for h in range(GROUP):
            fetch(go_hbm.at[s, :, pl.ds(h * 128, 128)], oh.at[s, pl.ds(h * 128, 128)])
    transpose(c)
    wk.step(0)
    wq.step(0)
    wk.step(1)
    wk.crossed(0)
    ya_r.wait_recv()
    y2a = net.send(xf.at[left, 0], xf.at[left, 0], "yr")
    yb_l.wait_recv()
    y2b = net.send(xf.at[right, 1], xf.at[right, 1], "yl")
    wq.step(1)
    wq.crossed(0)
    wk.step(2)
    wk.crossed(1)
    wq.step(2)
    wq.crossed(1)
    wk.step(3)
    wk.crossed(2)
    yb_r.wait_recv()
    ya_l.wait_recv()
    transpose(left)
    transpose(right)
    wq.step(3)
    wk.crossed(3)
    wq.crossed(2)
    wk.complete()

    settled = list(net.sent)

    def project(chunks, full, width):
        total = None
        for cc in chunks:
            w = full[pl.ds(2 * cc, 2)].reshape(DCOL, width)
            part = jnp.dot(xf[cc].reshape(TOK, DCOL), w, preferred_element_type=F32)
            total = part if total is None else total + part
        return total

    near = project((c, left, right), wkf, KVW)
    y2a.wait_recv()
    y2b.wait_recv()
    settled += [y2a, y2b]
    settled = [one for one in net.sent if any(one is copy for copy in settled)]
    near = (near + project((far,), wkf, KVW)).astype(BF16)

    def slot(zz, half):
        return kvb.at[zz, half, core]

    kvb[z, 0, core] = near[:SEQ_TOK]
    kvb[z, 1, core] = near[SEQ_TOK:]
    kvsib = {}

    def kv_arrived(s, k, half, ref):
        if s < 3:
            kvsib[k % RING, half] = net.send(ref, ref, "sib")

    kvsib[0, "a"] = net.send(slot(z, 0), slot(z, 0), "sib")
    kvsib[0, "b"] = net.send(slot(z, 1), slot(z, 1), "sib")
    kvboth = {}
    step = ring_gather(net, slot, 0, 1, kv_arrived, kvboth)

    wkv_got = []
    for i, (cc, name) in enumerate(((far, "yf"), (right, "yr"), (left, "yl"))):
        wkv_got.append(net.send(wkf.at[pl.ds(2 * cc, 2), core], wkv.at[i, core], name))
    transpose(far)
    for cc in (c, left, right, far):
        hand_round(cc)
    wq.crossed(3)
    step(0)
    wq.complete()
    query = project((c, left, right, far), wqf, QW).astype(BF16)
    for s in range(2):
        for h in range(GROUP):
            qh[s, h * 128 : (h + 1) * 128] = query[
                s * 128 : (s + 1) * 128, h * 128 : (h + 1) * 128
            ]
    for copy in local[4:]:
        copy.wait()

    def scores(s, zz):
        kv = kvb[zz, s].reshape(2 * SEQ_TOK, KVW)
        st = lax.dot_general(kv[:, :HEAD_DIM], qh[s], NT, preferred_element_type=F32)
        dp = lax.dot_general(kv[:, HEAD_DIM:], oh[s], NT, preferred_element_type=F32)
        return st * EXP_SCALE, dp

    def begin(s, carry):
        st, dp = scores(s, z)
        key = lax.broadcasted_iota(jnp.int32, (2 * SEQ_TOK, QW), 0)
        query_pos = lax.rem(lax.broadcasted_iota(jnp.int32, (2 * SEQ_TOK, QW), 1), SEQ_TOK)
        st = jnp.where(key <= query_pos + core * SEQ_TOK, st, -1e30)
        m = jnp.max(st, 0, keepdims=True)
        p = jnp.exp2(st - m)
        prob[z, s] = p
        gprob[z, s] = dp
        mblk[z, s] = m
        stat[s, 0:1] = m
        stat[s, 1:2] = jnp.sum(p, 0, keepdims=True)
        stat[s, 2:3] = jnp.sum(p * dp, 0, keepdims=True)
        return carry

    def more(zz):
        def one(s, carry):
            st, dp = scores(s, zz)
            old = stat[s, 0:1]
            m = jnp.maximum(old, jnp.max(st, 0, keepdims=True))
            p = jnp.exp2(st - m)
            fade = jnp.exp2(old - m)
            prob[zz, s] = p
            gprob[zz, s] = dp
            mblk[zz, s] = m
            stat[s, 0:1] = m
            stat[s, 1:2] = stat[s, 1:2] * fade + jnp.sum(p, 0, keepdims=True)
            stat[s, 2:3] = stat[s, 2:3] * fade + jnp.sum(p * dp, 0, keepdims=True)
            return carry

        @pl.when(zz < z)
        def _():
            lax.fori_loop(0, 2, one, 0)

    kvsib[0, "a"].wait_recv()
    kvsib[0, "b"].wait_recv()
    lax.fori_loop(0, 2, begin, 0)
    part[...] = jnp.zeros_like(part)
    dqt[...] = jnp.zeros_like(dqt)
    for s in range(4):
        if s:
            step(s)
        if s == 2:
            net.release(settled)
        for k in (-(s + 1), s + 1) if s < 3 else (4,):
            for half in ("a", "b"):
                if s < 3:
                    kvsib[k % RING, half].wait_recv()
                else:
                    kvboth["ra" if half == "a" else "lb"].wait_recv()
            more(net.zk(k))

    for s in range(2):
        inv = 1.0 / stat[s, 1:2]
        stat[s, 3:4] = inv
        stat[s, 4:5] = stat[s, 2:3] * inv

    def back_block(zz):
        for s in range(2):
            fac = jnp.exp2(mblk[zz, s] - stat[s, 0:1]) * stat[s, 3:4]
            p = prob[zz, s] * fac
            low = p.astype(BF16)
            ds = (p * (gprob[zz, s] - stat[s, 4:5])).astype(BF16)
            dv = jnp.dot(low, oh[s], preferred_element_type=F32)
            dk = jnp.dot(ds, qh[s], preferred_element_type=F32) * SCALE
            keys = kvb[zz, s].reshape(2 * SEQ_TOK, KVW)[:, :HEAD_DIM]
            dqt[s] += jnp.dot(keys.T, ds, preferred_element_type=F32)
            for co in range(2):
                part[zz, co, s, :, :HEAD_DIM] = dk[co * 128 : (co + 1) * 128].astype(BF16)
                part[zz, co, s, :, HEAD_DIM:] = dv[co * 128 : (co + 1) * 128].astype(BF16)

    swap = {}

    def back(n):
        def one(i, carry):
            zz = lax.rem(z + n + i * (2 * RING - 2 * n), RING)

            @pl.when(zz <= z)
            def _():
                back_block(zz)

            return carry

        ks = (n, -n) if n % 4 else (n,)
        lax.fori_loop(0, len(ks), one, 0)
        for k in ks if n % 4 or not n else ():
            swap[k] = net.send(part.at[net.zk(k), 1 - core], fromsib.at[net.zk(k)], "sib")

    def fold(k):
        swap[k].wait_recv()
        add(part.at[net.zk(k), core], fromsib.at[net.zk(k)])

    got = {}

    def out(way, half, n):
        got[way, half, n] = net.send(
            part.at[net.zk(n if way == "r" else -n), core, half],
            rin.at[0 if way == "r" else 1, half, n - 1],
            "zr" if way == "r" else "zl",
        )

    def take(way, half, n):
        got[way, half, n].wait_recv()
        add(
            part.at[net.zk(n - 1 if way == "r" else 1 - n), core, half],
            rin.at[0 if way == "r" else 1, half, n - 1],
        )

    def later(n):
        fold(n)
        fold(-n)
        for way, half in (("r", 1), ("l", 0), ("r", 0), ("l", 1)):
            take(way, half, n + 1)
            out(way, half, n)

    back(4)
    out("r", 0, 4)
    out("l", 1, 4)
    late = []
    for half, name in enumerate(("zrs", "zls")):
        late.append(net.send(part.at[net.zk(4), 1 - core, half], rlate.at[half], name))
    back(3)
    back(2)
    fold(3)
    fold(-3)
    out("r", 1, 3)
    out("l", 0, 3)
    back(1)
    back(0)

    for s in range(2):
        for h in range(GROUP):
            rq[0, s * 128 : (s + 1) * 128, h * 128 : (h + 1) * 128] = (
                (dqt[s, :, h * 128 : (h + 1) * 128] * SCALE).T.astype(BF16)
            )

    top, low = pl.ds(0, SEQ_TOK), pl.ds(SEQ_TOK, SEQ_TOK)
    rqa_r = net.send(rq.at[0, top], rq.at[2, top], "xr")
    rqb_l = net.send(rq.at[0, low], rq.at[3, low], "xl")
    rqb_r = net.send(rq.at[0, low], rq.at[2, low], "xr")
    rqa_l = net.send(rq.at[0, top], rq.at[3, top], "xl")

    def input_part(cc):
        w = wqf[pl.ds(2 * cc, 2)].reshape(DCOL, QW)
        return lax.dot_general(rq[0], w, NT, preferred_element_type=F32)

    def input_store(i, cc):
        xf[i] = input_part(cc).astype(BF16).reshape(2, SEQ_TOK, DCOL)

    to_far, to_right, to_left = xf.at[0], xf.at[1], xf.at[2]
    input_store(0, far)
    y0 = net.send(to_far.at[0], yin.at[0], "yr")
    y1 = net.send(to_far.at[1], yin.at[1], "yl")
    for way, half, k in (("r", 0, 3), ("l", 1, -3)):
        take(way, half, 4)
        late[half].wait_recv()
        add(part.at[net.zk(k), core, half], rlate.at[half])
        out(way, half, 3)
    input_store(1, right)
    y2 = net.send(to_right.at[1], yin.at[2], "yr")
    input_store(2, left)
    y3 = net.send(to_left.at[0], yin.at[3], "yl")

    wsq = RingSum(zqin, net, QW, xt, xg, rq, accq, dwq, dwqsib)
    wsk = DirectSum(zkin, net, KVW, xt, xg, rkx, acck, dwk, dwksib)
    wkv_sib = []
    for i, copy in enumerate(wkv_got):
        copy.wait_recv()
        wkv_sib.append(net.send(wkv.at[i, core], wkv.at[i, core], "sib"))
    wsq.multiply((0,), True, False)
    settled = [one for one in kvsib.values()] + list(kvboth.values())
    net.release(settled)
    later(2)
    rqa_r.wait_recv()
    rqa_f = net.send(rq.at[2, top], rq.at[1, top], "xr")
    rqb_l.wait_recv()
    rqb_f = net.send(rq.at[3, low], rq.at[1, low], "xl")
    later(1)
    y0.wait_recv()
    add(to_right.at[0], yin.at[0])
    y4 = net.send(to_right.at[0], yin.at[4], "yr")
    y1.wait_recv()
    add(to_left.at[1], yin.at[1])
    y5 = net.send(to_left.at[1], yin.at[5], "yl")
    total_own = input_part(c)
    fold(0)
    for half in range(2):
        total = part[z, core, half].astype(F32)
        for way in range(2):
            got["rl"[way], half, 1].wait_recv()
            total = total + rin[way, half, 0].astype(F32)
        rkx[0, half * 128 : (half + 1) * 128] = total.astype(BF16)
    rkx_got = [net.send(rkx.at[0], rkx.at[i + 1], ("xf", "xr", "xl")[i]) for i in range(3)]
    rky_got = [net.send(rkx.at[0], rky.at[i], ("yf", "yr", "yl")[i]) for i in range(3)]
    wsk.multiply((0,), True, False)
    for i in (1, 2):
        for copy in xg_got[i]:
            copy.wait_recv()
    rqb_r.wait_recv()
    rqa_l.wait_recv()
    wsq.multiply((2, 3), False, False)
    for copy in xg_got[0]:
        copy.wait_recv()
    rqa_f.wait_recv()
    rqb_f.wait_recv()
    wsq.multiply((1,), False, True)
    wsq.trade()
    wsq.start()
    for copy in wkv_sib:
        copy.wait_recv()
    total = total_own
    for i in (1, 2):
        rkx_got[i].wait_recv()
    wsk.multiply((2, 3), False, False)
    wsq.second()
    rkx_got[0].wait_recv()
    wsk.multiply((1,), False, True)
    wsk.trade()
    net.release([one for n in got for one in (got[n],)])
    net.release([one for copies in xg_got for one in copies] + wkv_got + wkv_sib + late)
    net.release(list(swap.values()) + [y0, y1, y2, y3, y4, y5, rqa_r, rqb_l, rqb_r, rqa_l])
    wsq.later(2)
    wsk.start()
    wsq.later(1)

    def key_share(rows, w):
        return lax.dot_general(rows, w.reshape(DCOL, KVW), NT, preferred_element_type=F32)

    total = total + key_share(rkx[0], wkf[pl.ds(2 * c, 2)])
    for i in range(3):
        rky_got[i].wait_recv()
        total = total + key_share(rky[i], jnp.stack([wkv[i, 0], wkv[i, 1]], 1))
    for copy in (y2, y3, y4, y5):
        copy.wait_recv()
    gi_ref[0] = (total[:SEQ_TOK] + yin[3].astype(F32) + yin[4].astype(F32)).astype(BF16)
    gi_ref[1] = (total[SEQ_TOK:] + yin[2].astype(F32) + yin[5].astype(F32)).astype(BF16)
    gkv = wsk.result()
    gk_ref[...] = gkv[:, :HEAD_DIM]
    gv_ref[...] = gkv[:, HEAD_DIM:]
    first, second = wsq.result()
    gq_ref[:32] = first
    gq_ref[32:] = second
    net.finish()
    assert net.count <= COPIES, net.count


def deliver_kernel(*refs):
    for src, dst in zip(refs[:4], refs[4:]):
        dst[...] = src[...]


def body(inputs, w_query, w_key, w_value, grad_out):
    vm = pl.BlockSpec(memory_space=pltpu.VMEM)
    hbm = pl.BlockSpec(memory_space=pltpu.HBM)
    results = pl.pallas_call(
        fused_kernel,
        name="fused",
        out_shape=(
            jax.ShapeDtypeStruct((2, SEQ_TOK, DCOL), BF16),
            jax.ShapeDtypeStruct((64, QW), F32),
            jax.ShapeDtypeStruct((64, HEAD_DIM), F32),
            jax.ShapeDtypeStruct((64, HEAD_DIM), F32),
        ),
        in_specs=[hbm] * 5,
        out_specs=(vm,) * 4,
        scratch_shapes=[
            pltpu.VMEM((COLS, 2, SEQ_TOK, DCOL), BF16),
            pltpu.VMEM((RING, 2, 4, 64, QW), BF16),
            pltpu.VMEM((RING, 2, 4, 64, KVW), BF16),
            pltpu.VMEM((RING, 2, 4, 64, TOK), BF16),
            pltpu.VMEM((RING, 2, 2, SEQ_TOK, KVW), BF16),
            pltpu.VMEM((2, QW, HEAD_DIM), BF16),
            pltpu.VMEM((2, QW, HEAD_DIM), BF16),
            pltpu.VMEM((RING, 2, 2 * SEQ_TOK, QW), F32),
            pltpu.VMEM((RING, 2, 2 * SEQ_TOK, QW), F32),
            pltpu.VMEM((RING, 2, 1, QW), F32),
            pltpu.VMEM((2, 8, QW), F32),
            pltpu.VMEM((2, HEAD_DIM, QW), F32),
            pltpu.VMEM((RING, 2, 2, SEQ_TOK, KVW), BF16),
            pltpu.VMEM((RING, 2, SEQ_TOK, KVW), BF16),
            pltpu.VMEM((2, 2, 4, SEQ_TOK, KVW), BF16),
            pltpu.VMEM((2, SEQ_TOK, KVW), BF16),
            pltpu.VMEM((DEPTHS, TOK, QW), BF16),
            pltpu.VMEM((DEPTHS, TOK, KVW), BF16),
            pltpu.VMEM((3, TOK, KVW), BF16),
            pltpu.VMEM((3, RING, 2, 64, TOK), BF16),
            pltpu.VMEM((3, 2, 2, 4, 64, KVW), BF16),
            pltpu.VMEM((6, SEQ_TOK, DCOL), BF16),
            pltpu.VMEM((RING, 2, 64, QW), F32),
            pltpu.VMEM((RING, 2, 64, QW), BF16),
            pltpu.VMEM((RING, 64, QW), BF16),
            pltpu.VMEM((2, 2, 4, 32, QW), BF16),
            pltpu.VMEM((RING, 2, 64, KVW), F32),
            pltpu.VMEM((RING, 2, 64, KVW), BF16),
            pltpu.VMEM((RING, 64, KVW), BF16),
            pltpu.VMEM((RING - 1, 64, KVW), BF16),
            pltpu.SemaphoreType.DMA((COPIES,)),
            pltpu.SemaphoreType.DMA((COPIES,)),
            pltpu.SemaphoreType.DMA((16,)),
        ],
        compiler_params=pltpu.CompilerParams(
            collective_id=0, has_side_effects=True, vmem_limit_bytes=57 << 20
        ),
    )(
        inputs,
        w_query.reshape(4, 64, QW),
        w_key.reshape(4, 64, HEAD_DIM),
        w_value.reshape(4, 64, HEAD_DIM),
        grad_out,
    )
    return pl.pallas_call(
        deliver_kernel,
        name="deliver",
        out_shape=[jax.ShapeDtypeStruct(one.shape, one.dtype) for one in results],
        in_specs=[vm] * 4,
        out_specs=[vm] * 4,
    )(*results)


def solution(mesh):
    return jax.shard_map(
        body,
        mesh=mesh,
        in_specs=(
            P("depth", "row", "col"),
            P("row", "col"),
            P("row", "col"),
            P("row", "col"),
            P("depth", "row", "col"),
        ),
        out_specs=(
            P("depth", "row", "col"),
            P(("row", "depth"), "col"),
            P(("row", "depth"), "col"),
            P(("row", "depth"), "col"),
        ),
        check_vma=False,
    )
```

```python
import functools

import jax
import jax.numpy as jnp
from jax import lax
from jax.experimental import pallas as pl
from jax.experimental.pallas import tpu as pltpu
from jax.sharding import PartitionSpec as P

HEAD_DIM = 128
ROWS, COLS, DEPTHS = 16, 4, 4
RING = ROWS // 2
TOK = 256
SEQ_TOK = 128
GROUP = 4
QW = 512
WIDTH = 768
KVW = 256
COPIES = 288
DCOL = 1024
TILE = 256
BF16, F32 = jnp.bfloat16, jnp.float32
SCALE = HEAD_DIM ** -0.5
EXP_SCALE = SCALE * 1.4426950408889634
NT = (((1,), (1,)), ((), ()))


class Net:
    def __init__(self, ssem, rsem):
        self.r = lax.axis_index("row")
        self.c = lax.axis_index("col")
        self.d = lax.axis_index("depth")
        self.z = self.r // 2
        self.core = lax.rem(self.r, 2)
        self.ssem, self.rsem = ssem, rsem
        self.count = 0
        self.sent = []
        self.peers = {
            "zr": {"row": lax.rem(self.r + 2, ROWS)},
            "zl": {"row": lax.rem(self.r + ROWS - 2, ROWS)},
            "sib": {"row": self.r + 1 - 2 * self.core},
            "yr": {"col": lax.rem(self.c + 1, COLS)},
            "yl": {"col": lax.rem(self.c + COLS - 1, COLS)},
            "yf": {"col": lax.rem(self.c + 2, COLS)},
            "xr": {"depth": lax.rem(self.d + 1, DEPTHS)},
            "xl": {"depth": lax.rem(self.d + DEPTHS - 1, DEPTHS)},
            "xf": {"depth": lax.rem(self.d + 2, DEPTHS)},
        }
        other = 1 - 2 * self.core
        self.peers["zrs"] = {"row": lax.rem(self.r + 2 + other, ROWS)}
        self.peers["zls"] = {"row": lax.rem(self.r + ROWS - 2 + other, ROWS)}
        for k in (2, 3, 4, 5, 6):
            self.peers["z%d" % k] = {"row": lax.rem(self.r + 2 * k, ROWS)}
        self.peers["z1"], self.peers["z7"] = self.peers["zr"], self.peers["zl"]

    def barrier(self, names):
        bar = pltpu.get_barrier_semaphore()
        for name in names:
            pl.semaphore_signal(
                bar, inc=1, device_id=self.peers[name], device_id_type=pl.DeviceIdType.MESH
            )
        pl.semaphore_wait(bar, len(names))

    def send(self, src, dst, name):
        i = self.count
        self.count += 1
        copy = pltpu.make_async_remote_copy(
            src_ref=src,
            dst_ref=dst,
            send_sem=self.ssem.at[i],
            recv_sem=self.rsem.at[i],
            device_id=self.peers[name],
            device_id_type=pl.DeviceIdType.MESH,
        )
        copy.start()
        self.sent.append(copy)
        return copy

    def release(self, copies):
        for copy in copies:
            copy.wait_send()
        self.sent = [one for one in self.sent if all(one is not copy for copy in copies)]

    def finish(self):
        for copy in self.sent:
            copy.wait_send()

    def zk(self, k):
        return lax.rem(self.z + k % RING, RING)


def ring_gather(net, slot, part_a, part_b, arrived, both=None):
    pend = {}
    pend["ra", 0] = net.send(slot(net.z, part_a), slot(net.z, part_a), "zr")
    pend["lb", 0] = net.send(slot(net.z, part_b), slot(net.z, part_b), "zl")
    pend["rb", 0] = net.send(slot(net.z, part_b), slot(net.z, part_b), "zr")
    pend["la", 0] = net.send(slot(net.z, part_a), slot(net.z, part_a), "zl")

    def step(s):
        for key, far in (("ra", 4), ("lb", 4), ("rb", 3), ("la", 3)):
            if s >= far:
                continue
            pend[key, s].wait_recv()
            k = -(s + 1) if key[0] == "r" else s + 1
            part = part_a if key[1] == "a" else part_b
            ref = slot(net.zk(k), part)
            if s + 1 < far:
                pend[key, s + 1] = net.send(ref, ref, "zr" if key[0] == "r" else "zl")
            if both is not None and s == 2 and far == 4:
                both[key] = net.send(ref, ref, "zrs" if key[0] == "r" else "zls")
            arrived(s, k, key[1], ref)

    return step


class WeightSum:
    def __init__(self, net, width, xt, xg, rows, acc, dw, dwsib):
        self.net, self.width, self.xt, self.xg, self.rows = net, width, xt, xg, rows
        self.acc, self.dw, self.dwsib = acc, dw, dwsib
        self.swap = {}

    def multiply(self, sources, first, last):
        def group(g, carry):
            at = pl.ds(2 * g, 2)
            total = None if first else self.acc[at].reshape(256, self.width)
            for i in sources:
                x = self.xg[i - 1, at] if i else self.xt[at, :, self.net.d]
                part = jnp.dot(x.reshape(256, TOK), self.rows[i], preferred_element_type=F32)
                total = part if total is None else total + part
            if last:
                self.dw[at] = total.astype(BF16).reshape(2, 2, 64, self.width)
            else:
                self.acc[at] = total.reshape(2, 2, 64, self.width)
            return carry

        lax.fori_loop(0, RING // 2, group, 0)

    def trade(self):
        net = self.net
        for k in (4, 3, -3, 2, -2, 1, -1, 0):
            zz = net.zk(k)
            self.swap[k] = net.send(self.dw.at[zz, 1 - net.core], self.dwsib.at[zz], "sib")

    def fold(self, k):
        zz = self.net.zk(k)
        self.swap[k].wait_recv()
        add(self.dw.at[zz, self.net.core], self.dwsib.at[zz])


class RingSum(WeightSum):
    def __init__(self, zin, *rest):
        super().__init__(*rest)
        self.zin, self.got = zin, {}

    def half(self, k, half):
        return self.dw.at[self.net.zk(k), self.net.core, pl.ds(32 * half, 32)]

    def out(self, way, half, n):
        self.got[way, half, n] = self.net.send(
            self.half(n if way == "r" else -n, half),
            self.zin.at[0 if way == "r" else 1, half, n - 1],
            "zr" if way == "r" else "zl",
        )

    def take(self, way, half, n):
        self.got[way, half, n].wait_recv()
        add(
            self.half(n - 1 if way == "r" else 1 - n, half),
            self.zin.at[0 if way == "r" else 1, half, n - 1],
        )

    def start(self):
        self.fold(4)
        self.out("r", 0, 4)
        self.out("l", 1, 4)
        self.fold(3)
        self.out("r", 1, 3)
        self.fold(-3)
        self.out("l", 0, 3)

    def second(self):
        self.take("r", 0, 4)
        self.out("r", 0, 3)
        self.take("l", 1, 4)
        self.out("l", 1, 3)

    def later(self, n):
        self.fold(n)
        self.fold(-n)
        for way, half in (("r", 1), ("l", 0), ("r", 0), ("l", 1)):
            self.take(way, half, n + 1)
            self.out(way, half, n)

    def result(self):
        self.fold(0)
        net, parts = self.net, []
        for half in range(2):
            total = self.half(0, half)[...].astype(F32)
            for way in range(2):
                self.got["rl"[way], half, 1].wait_recv()
                total = total + self.zin[way, half, 0].astype(F32)
            parts.append(total)
        return parts


class DirectSum(WeightSum):
    def __init__(self, zin, *rest):
        super().__init__(*rest)
        self.zin, self.got = zin, []

    def start(self):
        net = self.net
        for k in (4, 3, -3, 2, -2, 1, -1):
            self.fold(k)
            self.got.append(
                net.send(
                    self.dw.at[net.zk(k), net.core],
                    self.zin.at[k % RING - 1],
                    "z%d" % (k % RING),
                )
            )
        self.fold(0)

    def result(self):
        total = self.dw[self.net.z, self.net.core].astype(F32)
        for copy in self.got:
            copy.wait_recv()
        for i in range(RING - 1):
            total = total + self.zin[i].astype(F32)
        return total


def add(ref, src):
    ref[...] = (ref[...].astype(F32) + src[...].astype(F32)).astype(BF16)


def fused_kernel(
    x_hbm, wq_hbm, wk_hbm, wv_hbm, go_hbm, gi_ref, gq_ref, gk_ref, gv_ref,
    xf, wqf, wkf, xt, kvb, qh, oh, prob, gprob, mblk, stat, dqt, part, fromsib, rin, rlate,
    rq, rkx, rky, xg, wkv, yin, accq, dwq, dwqsib, zqin, acck, dwk, dwksib, zkin,
    ssem, rsem, lsem,
):
    net = Net(ssem, rsem)
    c, d, z, core = net.c, net.d, net.z, net.core
    left, right, far = lax.rem(c + 3, COLS), lax.rem(c + 1, COLS), lax.rem(c + 2, COLS)
    own_q, own_k = wqf.at[z, core], wkf.at[z, core]
    local = []

    def fetch(src, dst):
        copy = pltpu.make_async_copy(src, dst, lsem.at[len(local)])
        copy.start()
        local.append(copy)

    fetch(wk_hbm, own_k.at[:, :, pl.ds(0, 128)])
    fetch(wv_hbm, own_k.at[:, :, pl.ds(128, 128)])
    fetch(wq_hbm, own_q)
    fetch(x_hbm, xf.at[c])
    for s in range(2):
        for h in range(GROUP):
            fetch(go_hbm.at[s, :, pl.ds(h * 128, 128)], oh.at[s, pl.ds(h * 128, 128)])
    net.barrier(
        ["zr", "zl", "sib", "yr", "yl", "yf", "xr", "xl", "xf"]
        + ["z2", "z3", "z4", "z5", "z6", "zrs", "zls"]
    )
    for copy in local[:4]:
        copy.wait()

    class Spread:
        def __init__(self, full):
            self.full, self.sib, self.cross = full, [], {}
            own = full.at[z, core]
            self.step = ring_gather(
                net,
                lambda zz, q: full.at[zz, core, q],
                d,
                lax.rem(d + 1, DEPTHS),
                self.arrived,
            )
            self.sib.append(net.send(own, own, "sib"))

        def arrived(self, s, k, half, ref):
            self.cross[k, half] = net.send(ref, ref, "xr" if half == "a" else "xl")
            self.sib.append(net.send(ref, ref, "sib"))

        def crossed(self, s):
            for k in (-(s + 1), s + 1):
                for half in ("a", "b"):
                    if s == 3 and (k > 0) != (half == "b"):
                        continue
                    self.cross[k, half].wait_recv()
                    q = lax.rem(d + (3 if half == "a" else 2), DEPTHS)
                    ref = self.full.at[net.zk(k), core, q]
                    self.sib.append(net.send(ref, ref, "sib"))

        def complete(self):
            for copy in self.sib:
                copy.wait_recv()

    wk = Spread(wkf)
    ya_r = net.send(xf.at[c, 0], xf.at[c, 0], "yr")
    yb_l = net.send(xf.at[c, 1], xf.at[c, 1], "yl")
    yb_r = net.send(xf.at[c, 1], xf.at[c, 1], "yr")
    ya_l = net.send(xf.at[c, 0], xf.at[c, 0], "yl")
    wq = Spread(wqf)

    def transpose(cc):
        for s in range(2):
            for k in range(DCOL // 128):
                xt[
                    2 * cc + k // 4,
                    (k % 4) // 2,
                    2 * (k % 2) : 2 * (k % 2) + 2,
                    :,
                    s * 128 : (s + 1) * 128,
                ] = xf[cc, s, :, k * 128 : (k + 1) * 128].T.reshape(2, 64, 128)

    xg_got = [[], [], []]

    def hand_round(cc):
        for i, (n, name) in enumerate(((2, "xf"), (1, "xr"), (3, "xl"))):
            at = pl.ds(2 * cc, 2)
            quarter = lax.rem(d + n, DEPTHS)
            xg_got[i].append(net.send(xt.at[at, :, quarter], xg.at[i, at], name))

    transpose(c)
    wk.step(0)
    wq.step(0)
    wk.step(1)
    wk.crossed(0)
    ya_r.wait_recv()
    y2a = net.send(xf.at[left, 0], xf.at[left, 0], "yr")
    yb_l.wait_recv()
    y2b = net.send(xf.at[right, 1], xf.at[right, 1], "yl")
    wq.step(1)
    wq.crossed(0)
    wk.step(2)
    wk.crossed(1)
    wq.step(2)
    wq.crossed(1)
    wk.step(3)
    wk.crossed(2)
    yb_r.wait_recv()
    ya_l.wait_recv()
    transpose(left)
    transpose(right)
    wq.step(3)
    wk.crossed(3)
    wq.crossed(2)
    wk.complete()

    def project(chunks, full, width):
        total = None
        for cc in chunks:
            w = full[pl.ds(2 * cc, 2)].reshape(DCOL, width)
            part = jnp.dot(xf[cc].reshape(TOK, DCOL), w, preferred_element_type=F32)
            total = part if total is None else total + part
        return total

    near = project((c, left, right), wkf, KVW)
    y2a.wait_recv()
    y2b.wait_recv()
    near = (near + project((far,), wkf, KVW)).astype(BF16)

    def slot(zz, half):
        return kvb.at[zz, half, core]

    kvb[z, 0, core] = near[:SEQ_TOK]
    kvb[z, 1, core] = near[SEQ_TOK:]
    kvsib = {}

    def kv_arrived(s, k, half, ref):
        if s < 3:
            kvsib[k % RING, half] = net.send(ref, ref, "sib")

    kvsib[0, "a"] = net.send(slot(z, 0), slot(z, 0), "sib")
    kvsib[0, "b"] = net.send(slot(z, 1), slot(z, 1), "sib")
    kvboth = {}
    step = ring_gather(net, slot, 0, 1, kv_arrived, kvboth)

    wkv_got = []
    for i, (cc, name) in enumerate(((far, "yf"), (right, "yr"), (left, "yl"))):
        wkv_got.append(net.send(wkf.at[pl.ds(2 * cc, 2), core], wkv.at[i, core], name))
    transpose(far)
    for cc in (c, left, right, far):
        hand_round(cc)
    wq.crossed(3)
    step(0)
    wq.complete()
    query = project((c, left, right, far), wqf, QW).astype(BF16)
    for s in range(2):
        for h in range(GROUP):
            qh[s, h * 128 : (h + 1) * 128] = query[
                s * 128 : (s + 1) * 128, h * 128 : (h + 1) * 128
            ]
    for copy in local[4:]:
        copy.wait()
    net.release((ya_r, yb_l, yb_r, ya_l, y2a, y2b))

    def scores(s, zz):
        kv = kvb[zz, s].reshape(2 * SEQ_TOK, KVW)
        st = lax.dot_general(kv[:, :HEAD_DIM], qh[s], NT, preferred_element_type=F32)
        dp = lax.dot_general(kv[:, HEAD_DIM:], oh[s], NT, preferred_element_type=F32)
        return st * EXP_SCALE, dp

    def begin(s, carry):
        st, dp = scores(s, z)
        key = lax.broadcasted_iota(jnp.int32, (2 * SEQ_TOK, QW), 0)
        query_pos = lax.rem(lax.broadcasted_iota(jnp.int32, (2 * SEQ_TOK, QW), 1), SEQ_TOK)
        st = jnp.where(key <= query_pos + core * SEQ_TOK, st, -1e30)
        m = jnp.max(st, 0, keepdims=True)
        p = jnp.exp2(st - m)
        prob[z, s] = p
        gprob[z, s] = dp
        mblk[z, s] = m
        stat[s, 0:1] = m
        stat[s, 1:2] = jnp.sum(p, 0, keepdims=True)
        stat[s, 2:3] = jnp.sum(p * dp, 0, keepdims=True)
        return carry

    def more(zz):
        def one(s, carry):
            st, dp = scores(s, zz)
            old = stat[s, 0:1]
            m = jnp.maximum(old, jnp.max(st, 0, keepdims=True))
            p = jnp.exp2(st - m)
            fade = jnp.exp2(old - m)
            prob[zz, s] = p
            gprob[zz, s] = dp
            mblk[zz, s] = m
            stat[s, 0:1] = m
            stat[s, 1:2] = stat[s, 1:2] * fade + jnp.sum(p, 0, keepdims=True)
            stat[s, 2:3] = stat[s, 2:3] * fade + jnp.sum(p * dp, 0, keepdims=True)
            return carry

        @pl.when(zz < z)
        def _():
            lax.fori_loop(0, 2, one, 0)

    kvsib[0, "a"].wait_recv()
    kvsib[0, "b"].wait_recv()
    lax.fori_loop(0, 2, begin, 0)
    part[...] = jnp.zeros_like(part)
    dqt[...] = jnp.zeros_like(dqt)
    for s in range(4):
        if s:
            step(s)
        for k in (-(s + 1), s + 1) if s < 3 else (4,):
            for half in ("a", "b"):
                if s < 3:
                    kvsib[k % RING, half].wait_recv()
                else:
                    kvboth["ra" if half == "a" else "lb"].wait_recv()
            more(net.zk(k))

    for s in range(2):
        inv = 1.0 / stat[s, 1:2]
        stat[s, 3:4] = inv
        stat[s, 4:5] = stat[s, 2:3] * inv

    def back_block(zz):
        for s in range(2):
            fac = jnp.exp2(mblk[zz, s] - stat[s, 0:1]) * stat[s, 3:4]
            p = prob[zz, s] * fac
            low = p.astype(BF16)
            ds = (p * (gprob[zz, s] - stat[s, 4:5])).astype(BF16)
            dv = jnp.dot(low, oh[s], preferred_element_type=F32)
            dk = jnp.dot(ds, qh[s], preferred_element_type=F32) * SCALE
            keys = kvb[zz, s].reshape(2 * SEQ_TOK, KVW)[:, :HEAD_DIM]
            dqt[s] += jnp.dot(keys.T, ds, preferred_element_type=F32)
            for co in range(2):
                part[zz, co, s, :, :HEAD_DIM] = dk[co * 128 : (co + 1) * 128].astype(BF16)
                part[zz, co, s, :, HEAD_DIM:] = dv[co * 128 : (co + 1) * 128].astype(BF16)

    swap = {}

    def back(n):
        def one(i, carry):
            zz = lax.rem(z + n + i * (2 * RING - 2 * n), RING)

            @pl.when(zz <= z)
            def _():
                back_block(zz)

            return carry

        ks = (n, -n) if n % 4 else (n,)
        lax.fori_loop(0, len(ks), one, 0)
        for k in ks if n % 4 or not n else ():
            swap[k] = net.send(part.at[net.zk(k), 1 - core], fromsib.at[net.zk(k)], "sib")

    def fold(k):
        swap[k].wait_recv()
        add(part.at[net.zk(k), core], fromsib.at[net.zk(k)])

    got = {}

    def out(way, half, n):
        got[way, half, n] = net.send(
            part.at[net.zk(n if way == "r" else -n), core, half],
            rin.at[0 if way == "r" else 1, half, n - 1],
            "zr" if way == "r" else "zl",
        )

    def take(way, half, n):
        got[way, half, n].wait_recv()
        add(
            part.at[net.zk(n - 1 if way == "r" else 1 - n), core, half],
            rin.at[0 if way == "r" else 1, half, n - 1],
        )

    def later(n):
        fold(n)
        fold(-n)
        for way, half in (("r", 1), ("l", 0), ("r", 0), ("l", 1)):
            take(way, half, n + 1)
            out(way, half, n)

    back(4)
    out("r", 0, 4)
    out("l", 1, 4)
    late = []
    for half, name in enumerate(("zrs", "zls")):
        late.append(net.send(part.at[net.zk(4), 1 - core, half], rlate.at[half], name))
    back(3)
    back(2)
    fold(3)
    fold(-3)
    out("r", 1, 3)
    out("l", 0, 3)
    back(1)
    back(0)

    for s in range(2):
        for h in range(GROUP):
            rq[0, s * 128 : (s + 1) * 128, h * 128 : (h + 1) * 128] = (
                (dqt[s, :, h * 128 : (h + 1) * 128] * SCALE).T.astype(BF16)
            )

    top, low = pl.ds(0, SEQ_TOK), pl.ds(SEQ_TOK, SEQ_TOK)
    rqa_r = net.send(rq.at[0, top], rq.at[2, top], "xr")
    rqb_l = net.send(rq.at[0, low], rq.at[3, low], "xl")
    rqb_r = net.send(rq.at[0, low], rq.at[2, low], "xr")
    rqa_l = net.send(rq.at[0, top], rq.at[3, top], "xl")

    def input_part(cc):
        w = wqf[pl.ds(2 * cc, 2)].reshape(DCOL, QW)
        return lax.dot_general(rq[0], w, NT, preferred_element_type=F32)

    def input_store(i, cc):
        xf[i] = input_part(cc).astype(BF16).reshape(2, SEQ_TOK, DCOL)

    to_far, to_right, to_left = xf.at[0], xf.at[1], xf.at[2]
    input_store(0, far)
    y0 = net.send(to_far.at[0], yin.at[0], "yr")
    y1 = net.send(to_far.at[1], yin.at[1], "yl")
    for way, half, k in (("r", 0, 3), ("l", 1, -3)):
        take(way, half, 4)
        late[half].wait_recv()
        add(part.at[net.zk(k), core, half], rlate.at[half])
        out(way, half, 3)
    input_store(1, right)
    y2 = net.send(to_right.at[1], yin.at[2], "yr")
    input_store(2, left)
    y3 = net.send(to_left.at[0], yin.at[3], "yl")

    wsq = RingSum(zqin, net, QW, xt, xg, rq, accq, dwq, dwqsib)
    wsk = DirectSum(zkin, net, KVW, xt, xg, rkx, acck, dwk, dwksib)
    wkv_sib = []
    for i, copy in enumerate(wkv_got):
        copy.wait_recv()
        wkv_sib.append(net.send(wkv.at[i, core], wkv.at[i, core], "sib"))
    wsq.multiply((0,), True, False)
    later(2)
    rqa_r.wait_recv()
    rqa_f = net.send(rq.at[2, top], rq.at[1, top], "xr")
    rqb_l.wait_recv()
    rqb_f = net.send(rq.at[3, low], rq.at[1, low], "xl")
    later(1)
    y0.wait_recv()
    add(to_right.at[0], yin.at[0])
    y4 = net.send(to_right.at[0], yin.at[4], "yr")
    y1.wait_recv()
    add(to_left.at[1], yin.at[1])
    y5 = net.send(to_left.at[1], yin.at[5], "yl")
    total_own = input_part(c)
    fold(0)
    for half in range(2):
        total = part[z, core, half].astype(F32)
        for way in range(2):
            got["rl"[way], half, 1].wait_recv()
            total = total + rin[way, half, 0].astype(F32)
        rkx[0, half * 128 : (half + 1) * 128] = total.astype(BF16)
    rkx_got = [net.send(rkx.at[0], rkx.at[i + 1], ("xf", "xr", "xl")[i]) for i in range(3)]
    rky_got = [net.send(rkx.at[0], rky.at[i], ("yf", "yr", "yl")[i]) for i in range(3)]
    wsk.multiply((0,), True, False)
    for i in (1, 2):
        for copy in xg_got[i]:
            copy.wait_recv()
    rqb_r.wait_recv()
    rqa_l.wait_recv()
    wsq.multiply((2, 3), False, False)
    for copy in xg_got[0]:
        copy.wait_recv()
    rqa_f.wait_recv()
    rqb_f.wait_recv()
    wsq.multiply((1,), False, True)
    wsq.trade()
    wsq.start()
    for copy in wkv_sib:
        copy.wait_recv()
    total = total_own
    for i in (1, 2):
        rkx_got[i].wait_recv()
    wsk.multiply((2, 3), False, False)
    wsq.second()
    rkx_got[0].wait_recv()
    wsk.multiply((1,), False, True)
    wsk.trade()
    wsq.later(2)
    wsk.start()
    wsq.later(1)

    def key_share(rows, w):
        return lax.dot_general(rows, w.reshape(DCOL, KVW), NT, preferred_element_type=F32)

    total = total + key_share(rkx[0], wkf[pl.ds(2 * c, 2)])
    for i in range(3):
        rky_got[i].wait_recv()
        total = total + key_share(rky[i], jnp.stack([wkv[i, 0], wkv[i, 1]], 1))
    for copy in (y2, y3, y4, y5):
        copy.wait_recv()
    xf[3, 0] = (total[:SEQ_TOK] + yin[3].astype(F32) + yin[4].astype(F32)).astype(BF16)
    xf[3, 1] = (total[SEQ_TOK:] + yin[2].astype(F32) + yin[5].astype(F32)).astype(BF16)
    gi_out = pltpu.make_async_copy(xf.at[3], gi_ref, lsem.at[len(local)])
    gi_out.start()
    gkv = wsk.result()
    gk_ref[...] = gkv[:, :HEAD_DIM]
    gv_ref[...] = gkv[:, HEAD_DIM:]
    first, second = wsq.result()
    gq_ref[:32] = first
    gq_ref[32:] = second
    net.finish()
    gi_out.wait()
    assert net.count <= COPIES, net.count


def deliver_kernel(*refs):
    for src, dst in zip(refs[:4], refs[4:]):
        dst[...] = src[...]


def body(inputs, w_query, w_key, w_value, grad_out):
    vm = pl.BlockSpec(memory_space=pltpu.VMEM)
    hbm = pl.BlockSpec(memory_space=pltpu.HBM)
    results = pl.pallas_call(
        fused_kernel,
        name="fused",
        out_shape=(
            jax.ShapeDtypeStruct((2, SEQ_TOK, DCOL), BF16),
            jax.ShapeDtypeStruct((64, QW), F32),
            jax.ShapeDtypeStruct((64, HEAD_DIM), F32),
            jax.ShapeDtypeStruct((64, HEAD_DIM), F32),
        ),
        in_specs=[hbm] * 5,
        out_specs=(hbm, vm, vm, vm),
        scratch_shapes=[
            pltpu.VMEM((COLS, 2, SEQ_TOK, DCOL), BF16),
            pltpu.VMEM((RING, 2, 4, 64, QW), BF16),
            pltpu.VMEM((RING, 2, 4, 64, KVW), BF16),
            pltpu.VMEM((RING, 2, 4, 64, TOK), BF16),
            pltpu.VMEM((RING, 2, 2, SEQ_TOK, KVW), BF16),
            pltpu.VMEM((2, QW, HEAD_DIM), BF16),
            pltpu.VMEM((2, QW, HEAD_DIM), BF16),
            pltpu.VMEM((RING, 2, 2 * SEQ_TOK, QW), F32),
            pltpu.VMEM((RING, 2, 2 * SEQ_TOK, QW), F32),
            pltpu.VMEM((RING, 2, 1, QW), F32),
            pltpu.VMEM((2, 8, QW), F32),
            pltpu.VMEM((2, HEAD_DIM, QW), F32),
            pltpu.VMEM((RING, 2, 2, SEQ_TOK, KVW), BF16),
            pltpu.VMEM((RING, 2, SEQ_TOK, KVW), BF16),
            pltpu.VMEM((2, 2, 4, SEQ_TOK, KVW), BF16),
            pltpu.VMEM((2, SEQ_TOK, KVW), BF16),
            pltpu.VMEM((DEPTHS, TOK, QW), BF16),
            pltpu.VMEM((DEPTHS, TOK, KVW), BF16),
            pltpu.VMEM((3, TOK, KVW), BF16),
            pltpu.VMEM((3, RING, 2, 64, TOK), BF16),
            pltpu.VMEM((3, 2, 2, 4, 64, KVW), BF16),
            pltpu.VMEM((6, SEQ_TOK, DCOL), BF16),
            pltpu.VMEM((RING, 2, 64, QW), F32),
            pltpu.VMEM((RING, 2, 64, QW), BF16),
            pltpu.VMEM((RING, 64, QW), BF16),
            pltpu.VMEM((2, 2, 4, 32, QW), BF16),
            pltpu.VMEM((RING, 2, 64, KVW), F32),
            pltpu.VMEM((RING, 2, 64, KVW), BF16),
            pltpu.VMEM((RING, 64, KVW), BF16),
            pltpu.VMEM((RING - 1, 64, KVW), BF16),
            pltpu.SemaphoreType.DMA((COPIES,)),
            pltpu.SemaphoreType.DMA((COPIES,)),
            pltpu.SemaphoreType.DMA((16,)),
        ],
        compiler_params=pltpu.CompilerParams(
            collective_id=0, has_side_effects=True, vmem_limit_bytes=57 << 20
        ),
    )(
        inputs,
        w_query.reshape(4, 64, QW),
        w_key.reshape(4, 64, HEAD_DIM),
        w_value.reshape(4, 64, HEAD_DIM),
        grad_out,
    )
    return pl.pallas_call(
        deliver_kernel,
        name="deliver",
        out_shape=[jax.ShapeDtypeStruct(one.shape, one.dtype) for one in results],
        in_specs=[vm] * 4,
        out_specs=[vm] * 4,
    )(*results)


def solution(mesh):
    return jax.shard_map(
        body,
        mesh=mesh,
        in_specs=(
            P("depth", "row", "col"),
            P("row", "col"),
            P("row", "col"),
            P("row", "col"),
            P("depth", "row", "col"),
        ),
        out_specs=(
            P("depth", "row", "col"),
            P(("row", "depth"), "col"),
            P(("row", "depth"), "col"),
            P(("row", "depth"), "col"),
        ),
        check_vma=False,
    )
```
